128 devices in a mesh: dp: 4 (over x), rows: 2 (over core), vocab: 16 (over z, y).
Axes of the slice: x: 4, y: 4, z: 4, core: 2. Of those that a mesh axis runs over, the one named last changes fastest.
Arguments:
- hidden: bfloat16 [1024, 8192], P('vocab', ('dp', 'rows')), may hold values from -150 to 150
- head: bfloat16 [8192, 65536], P(('dp', 'rows'), 'vocab'), may hold values from -0.0625 to 0.0625
- ref_logits: bfloat16 [1024, 65536], P(('dp', 'rows'), 'vocab'), may hold values from -200 to 200
- token_ids: int32 [1024], replicated, may hold values from 0 to 65535
- group_ids: int32 [1024], replicated, may hold values from 0 to 63
- response_mask: int32 [1024], replicated, may hold values 0 or 1
- advantages: float32 [64], replicated, may hold values from -4 to 4
Outputs:
- hidden_grad: float32 [1024, 8192], P('vocab', ('dp', 'rows'))
- head_grad: float32 [8192, 65536], P(('dp', 'rows'), 'vocab')
The draws below stay inside these ranges and needn't reach their ends.
All inputs are finite; a program needn't handle non-finite values.
Results may differ from the reference program's by a relative error of at most 0.0031.
Values may be sent and summed in bfloat16 or wider, within the bound.
A program may use at most 128 MiB of HBM per device.

```python
import math
import jax
import jax.numpy as jnp
import numpy as np

D = 8192
GROUPS = 64
TOKENS = 1024
VOCAB = 65536


def draw_hidden(key, part):
    key = jax.random.fold_in(key, 11)
    second = jax.random.fold_in(key, 1)
    values = 3.0 * jnp.clip(jax.random.normal(second, (TOKENS, D), jnp.float32), -4.0, 4.0)
    return values.astype(jnp.bfloat16)


def draw_ref_logits(key, part):
    key = jax.random.fold_in(key, 23)
    second = jax.random.fold_in(key, 1)
    values = 3.0 * jnp.clip(jax.random.normal(second, (TOKENS, VOCAB), jnp.float32), -4.0, 4.0)
    return values.astype(jnp.bfloat16)


def with_ends(drawn, own_key, least, high):
    longest = drawn.shape.index(max(drawn.shape))
    spots = []
    for shift in (0, 1):
        where = [jax.random.randint(jax.random.fold_in(own_key, axis), (), 0, length) for axis, length in enumerate(drawn.shape)]
        where[longest] = (where[longest] + shift) % drawn.shape[longest]
        spots.append(tuple(where))
    return drawn.at[spots[0]].set(least).at[spots[1]].set(high)


def shard_levels(stream_key, dims, cuts, smallest, high):
    def one(dim, blocks):
        draws = jax.random.uniform(jax.random.fold_in(jax.random.fold_in(stream_key, 6), dim), (blocks,), jnp.float32, smallest / len(cuts), high / len(cuts))
        return jnp.repeat(jnp.exp(draws), dims[dim] // blocks).reshape((-1,) + (1,) * (len(dims) - dim - 1))

    gain = one(*cuts[0])
    for cut in cuts[1:]:
        gain = gain * one(*cut)
    return gain


def cumulative_ranks(amount, lean):
    portions = [(1 << 20) // math.isqrt(rank ** lean) + 1 for rank in range(1, amount + 1)]
    width = 1 + sum(portions) // (1 << 30)
    return np.cumsum(np.array([max(1, weight // width) for weight in portions]))


def ranked_ids(stream_key, shape, number_of, slope):
    table = cumulative_ranks(number_of, slope)
    ticket = jax.random.randint(jax.random.fold_in(stream_key, 1), shape, 0, int(table[number_of - 1]))
    rank = jnp.searchsorted(jnp.asarray(table, jnp.int32), ticket, side="right")
    return jax.random.permutation(jax.random.fold_in(stream_key, 2), number_of)[rank].astype(jnp.int32)


def scatter_about(own_key, extent, spread, most, cuts=(), held_as=jnp.bfloat16):
    gain = shard_levels(own_key, extent, cuts, -0.22, 0.18) if cuts else 1.0
    entries = jax.random.normal(own_key, extent, jnp.float32) * spread * gain
    return jnp.minimum(jnp.maximum(entries, -most), most).astype(held_as)


def setup_inputs(seed: int = 0) -> dict:
    key_of = jax.random.split(jax.random.key(seed), 8)
    return {
        "hidden": draw_hidden(jax.random.fold_in(key_of[7], 71), 0),
        "head": scatter_about(key_of[1], (D, VOCAB), D ** -0.5, 0.0625, ((0, 8), (1, 16))),
        "ref_logits": draw_ref_logits(jax.random.fold_in(key_of[7], 71), 0),
        "token_ids": with_ends(ranked_ids(key_of[3], (TOKENS,), VOCAB, 2), jax.random.fold_in(key_of[3], 3), 0, VOCAB - 1).astype(jnp.int32),
        "group_ids": with_ends(jax.random.randint(key_of[4], (TOKENS,), 0, GROUPS), jax.random.fold_in(key_of[4], 1), 0, GROUPS - 1).astype(jnp.int32),
        "response_mask": with_ends((jax.random.randint(key_of[5], (TOKENS,), 0, 4) < 3).astype(jnp.int32), jax.random.fold_in(key_of[5], 1), 0, 1),
        "advantages": scatter_about(key_of[6], (GROUPS,), 1.0, 4.0, (), jnp.float32),
    }


def reference(hidden, head, ref_logits, token_ids, group_ids, response_mask, advantages):
    logits = jnp.dot(hidden, head, preferred_element_type=jnp.float32)
    refs = ref_logits.astype(jnp.float32)
    top = jnp.max(logits, axis=1, keepdims=True)
    expo = jnp.exp(logits - top)
    total = jnp.sum(expo, axis=1, keepdims=True)
    lse = top + jnp.log(total)
    qtop = jnp.max(refs, axis=1, keepdims=True)
    qlse = qtop + jnp.log(jnp.sum(jnp.exp(refs - qtop), axis=1, keepdims=True))
    mean_z = jnp.sum(expo * logits, axis=1, keepdims=True) / total
    mean_r = jnp.sum(expo * refs, axis=1, keepdims=True) / total
    kl_term = mean_z - mean_r - lse + qlse
    entropy = lse - mean_z
    log_p = logits - lse
    log_q = refs - qlse
    probs = jnp.exp(log_p)
    adv = advantages[group_ids][:, None]
    columns = jnp.arange(logits.shape[1], dtype=jnp.int32)
    pick = (token_ids[:, None] == columns[None, :]).astype(jnp.float32)
    weight = response_mask.astype(jnp.float32)[:, None]
    dlogits = weight * (adv * (probs - pick) + 0.04 * probs * (log_p - log_q - kl_term) + 0.02 * probs * (log_p + entropy))
    dlogits = dlogits.astype(jnp.bfloat16)
    hidden_grad = jnp.dot(dlogits, head.T, preferred_element_type=jnp.float32)
    head_grad = jnp.dot(hidden.T, dlogits, preferred_element_type=jnp.float32)
    return hidden_grad, head_grad
```

```python
import functools

import jax
import jax.numpy as jnp
from jax import lax
from jax.experimental import pallas as pl
from jax.experimental.pallas import tpu as pltpu
from jax.sharding import PartitionSpec as P

MESH = pl.DeviceIdType.MESH
CHUNKS = 4
NX = 4
NY = 4
NZ = 4
ROWS = 16
SUBS = 2
TILE = 2048
MTILE = 1024
PTILE = 512
LANES = 128
UNIT = 32000.0
F32 = jnp.float32
SENDERS = ("core0", "core1", "h1", "h2", "q1", "q2", "s", "g1y", "g1z", "g2", "c", "a")

ORDER = (
    "A0", "B0", "A1", "B1", "M0", "Q0", "M1", "A2", "Q1", "R0", "B2", "R1", "A3", "Q2", "L0", "B3", "Q3",
    "R2", "S0", "L1", "R3", "M2", "T0", "S1", "L2", "Q4", "F0", "T1", "Q5", "L3", "R4", "M3", "S2", "S3",
    "F1", "Q6", "T2", "L4", "R5", "Q7", "C0", "C1", "R6", "S4", "P0", "T3", "L5", "F2", "R7", "L6", "S5",
    "F3", "T4", "S6", "T5", "C2", "L7", "T6", "C3", "U0", "S7", "F4", "P1", "F5", "T7", "V0", "C4", "C5",
    "F6", "U1", "F7", "P2", "C6", "C7", "P3", "U2", "V1", "U3", "V2", "V3",
)


def fold(values):
    return [values[:, j : j + LANES] for j in range(0, values.shape[1], LANES)]


def column(row):
    square = (LANES, LANES)
    same = lax.broadcasted_iota(jnp.int32, square, 0) == lax.broadcasted_iota(jnp.int32, square, 1)
    return jnp.sum(jnp.where(same, jnp.broadcast_to(row, square), 0.0), axis=1, keepdims=True)


def spread(columns):
    rows = columns[0].shape[0]
    lane = lax.broadcasted_iota(jnp.int32, (rows, LANES), 1)
    tile = jnp.zeros((rows, LANES), F32)
    for j, value in enumerate(columns):
        tile = jnp.where(lane == j, value, tile)
    return tile


def merge(tiles):
    get = lambda tile, j: tile[:, j : j + 1]
    top = functools.reduce(jnp.maximum, [get(t, 0) for t in tiles])
    qtop = functools.reduce(jnp.maximum, [get(t, 4) for t in tiles])
    scale = [jnp.exp(get(t, 0) - top) for t in tiles]
    qscale = [jnp.exp(get(t, 4) - qtop) for t in tiles]
    total, sum_z, sum_r = (sum(get(t, j) * s for t, s in zip(tiles, scale)) for j in (1, 2, 3))
    qtotal = sum(get(t, 5) * s for t, s in zip(tiles, qscale))
    return (top, total, sum_z, sum_r, qtop, qtotal)


def kernel(
    hidden_ref, head_ref, refs_ref, token_ref, group_ref, mask_ref, adv_ref,
    hgrad_ref, dl_out, hid_out,
    head, hid, refs, part, crecv, temp, q1s, q1r, q2s, q2r, zbuf, stat_s, stat_r, dl, pg, ra, rsum, rb,
    tok_c, adv_c, wgt_c, send_sem, recv_sem, local_sem,
):
    x = lax.axis_index("dp")
    core = lax.axis_index("rows")
    shard = lax.axis_index("vocab")
    y, z = lax.rem(shard, NY), lax.div(shard, NY)
    width = head.shape[1]
    half = width // 2
    depth = head.shape[0]
    dhalf = depth // 2
    block = 2 * x + core
    ycd, ylo = lax.div(y, 2), lax.rem(y, 2)

    def xof(step):
        return lax.rem(x + step + 2 * NX, NX)

    def yof(step):
        return lax.rem(y + step, NY)

    def zof(step):
        return lax.rem(z + step, NZ)

    def at_core():
        return {"rows": 1 - core}

    def at_x(step):
        return {"dp": xof(step)}

    def at_y(step):
        return {"vocab": z * NY + yof(step)}

    def at_z(step):
        return {"vocab": zof(step) * NY + y}

    numbers = {}

    def number(key):
        if key[1] in ("q1", "q2", "a+", "a-", "a"):
            return numbers.setdefault(key, len(numbers))
        if key[1] == "c":
            return numbers.setdefault((key[0] // SUBS, "c"), len(numbers))
        return numbers.setdefault(key[:2], len(numbers))

    def send(key, src, dst, device):
        name = key[1] + str(key[0] % 2) if key[1] == "core" else key[1]
        n = next(i for i, start in enumerate(SENDERS) if name.startswith(start))
        pltpu.make_async_remote_copy(
            src_ref=src, dst_ref=dst, send_sem=send_sem.at[n], recv_sem=recv_sem.at[number(key)],
            device_id=device, device_id_type=MESH,
        ).start()

    def arrive(key, view):
        pltpu.make_async_copy(view, view, recv_sem.at[number(key)]).wait()

    def sent(name, view):
        pltpu.make_async_copy(view, view, send_sem.at[SENDERS.index(name)]).wait()

    locals_ = []

    def bring(src, dst):
        copy = pltpu.make_async_copy(src, dst, local_sem.at[len(locals_)])
        copy.start()
        locals_.append(copy)
        return copy

    own = [bring(hidden_ref.at[pl.ds(ROWS * k, ROWS)], hid.at[k, ycd, z, ylo]) for k in range(CHUNKS)]
    head_loads = [
        bring(head_ref.at[pl.ds(j * depth // 4, depth // 4)], head.at[pl.ds(j * depth // 4, depth // 4)])
        for j in range(4)
    ]
    refs_load = bring(refs_ref, refs)
    barrier = pltpu.get_barrier_semaphore()
    peers = [at_core(), at_x(1), at_x(-1)] + [at_y(d) for d in (1, 2, 3)] + [at_z(d) for d in (1, 2, 3)]
    for peer in peers:
        pl.semaphore_signal(barrier, inc=1, device_id=peer, device_id_type=MESH)
    pl.semaphore_wait(barrier, len(peers))

    cols0, cols1 = pl.ds(0, dhalf), pl.ds(dhalf, dhalf)
    def own_row(ref):
        values = ref[...].astype(F32)
        at = lax.broadcasted_iota(jnp.int32, values.shape, 0) == block
        return jnp.sum(jnp.where(at, values, 0.0), axis=0, keepdims=True)

    groups = adv_ref.shape[1]
    group_col = column(own_row(group_ref))
    group_at = lax.broadcasted_iota(jnp.int32, (LANES, groups), 1).astype(F32)
    adv_col = jnp.sum(jnp.where(group_col == group_at, adv_ref[...], 0.0), axis=1, keepdims=True)
    tok_c[...] = jnp.broadcast_to(column(own_row(token_ref)), tok_c.shape)
    adv_c[...] = jnp.broadcast_to(adv_col, adv_c.shape)
    wgt_c[...] = jnp.broadcast_to(column(own_row(mask_ref)), wgt_c.shape)

    def own_rows(ref, k, cols):
        at = 4 * ROWS * (k % SUBS) + ROWS * (k // SUBS)
        return ref[pl.ds(at, ROWS), cols].astype(F32)

    def tiles(lo, hi, body, init):
        def step(i, carry):
            return body(pl.multiple_of(i * TILE, TILE), carry)

        return lax.fori_loop(lo // TILE, hi // TILE, step, init)

    def exponent(top):
        return jnp.floor(jnp.log2(jnp.maximum(top, 1e-30))) + 1.0

    def code(values, by):
        return jnp.round(values * by).astype(jnp.int32).astype(jnp.int16)

    def decode(ref, cols, by):
        return ref[:, cols].astype(jnp.int32).astype(F32) * by

    def unit_of(ref, at):
        return jnp.exp2(ref[:, pl.ds(at, LANES)].astype(jnp.int32).astype(F32)[:, 0:1]) * (1.0 / UNIT)

    def local_sum(k, xd, cols):
        c, low = k // SUBS, k % SUBS
        return part[c % 2, core, xd, low, :, cols] + crecv[c, xd, low, :, cols]

    def stage_a(k):
        own[k].wait()
        for d in (1, 3, 2):
            mine = hid.at[k, ycd, z, ylo, :, cols0]
            send((k, "h1y", d), mine, mine, at_y(d))
            mine = hid.at[k, ycd, z, ylo, :, cols1]
            send((k, "h1z", d), mine, mine, at_z(d))

    def stage_b(k):
        arrive((k, "h1y"), dl.at[0, 0, pl.ds(0, 3), 0, :, cols0])
        arrive((k, "h1z"), dl.at[0, 0, pl.ds(0, 3), 0, :, cols0])
        for d in (1, 3, 2):
            mine = hid.at[k, :, z, :, :, cols0]
            send((k, "h2z", d), mine, mine, at_z(d))
            mine = hid.at[k, ycd, :, ylo, :, cols1]
            send((k, "h2y", d), mine, mine, at_y(d))

    def stage_m(k):
        if k == 0:
            for copy in head_loads:
                copy.wait()
        arrive((k, "h2z"), dl.at[0, :, pl.ds(0, 3), :, :, cols0])
        arrive((k, "h2y"), dl.at[0, :, pl.ds(0, 3), :, :, cols0])
        bring(hid.at[k], hid_out.at[k])
        slot = k % 2
        if k >= 2:
            sent("core" + str(slot), part.at[slot, 1 - core])
        span = width // 4
        for g in range(4):
            def step(i, carry):
                cols = pl.ds(pl.multiple_of(g * span + i * MTILE, MTILE), MTILE)
                rows = hid[k].reshape(16 * ROWS, depth)
                out = jnp.dot(rows, head[:, cols], preferred_element_type=F32)
                part[slot, :, :, :, :, cols] = out.reshape(2, NX, SUBS, ROWS, MTILE)
                return carry

            lax.fori_loop(0, span // MTILE, step, 0)
            cols = pl.ds(g * span, span)
            send((k, "core", g), part.at[slot, 1 - core, :, :, :, cols], crecv.at[k, :, :, :, cols], at_core())

    def stage_q(k):
        if k % SUBS == 0:
            arrive((k // SUBS, "core"), crecv.at[k // SUBS])
        xd = xof(2)

        def first(at, top):
            cols = pl.ds(at, TILE)
            value = local_sum(k, xd, cols)
            temp[:, cols] = value
            return functools.reduce(jnp.maximum, fold(jnp.abs(value)), top)

        top = tiles(0, width, first, jnp.zeros((ROWS, LANES), F32))
        power = exponent(jnp.max(top, axis=1, keepdims=True))
        by = jnp.exp2(-power) * UNIT
        for j in range(2):

            def second(at, carry):
                q1s[k, j, :, pl.ds(pl.multiple_of(at - j * half, TILE), TILE)] = code(temp[:, pl.ds(at, TILE)], by)
                return carry

            tiles(j * half, (j + 1) * half, second, 0)
            q1s[k, j, :, pl.ds(half, LANES)] = jnp.broadcast_to(power, (ROWS, LANES)).astype(jnp.int32).astype(jnp.int16)
            send((k, "q1", j), q1s.at[k, j], q1r.at[k, j], at_x(1 if j == 0 else -1))

    def stage_r(k):
        for j in range(2):
            step = 1 if j == 0 else -1
            xd = xof(step)
            arrive((k, "q1", j), q1r.at[k, j])
            unit = unit_of(q1r.at[k, j], half)

            def plain(at, top):
                cols = pl.ds(at, TILE)
                value = local_sum(k, xd, cols)
                temp[:, cols] = value
                return functools.reduce(jnp.maximum, fold(jnp.abs(value)), top)

            def passing(at, top):
                cols = pl.ds(at, TILE)
                value = local_sum(k, xd, cols)
                value += decode(q1r.at[k, j], pl.ds(pl.multiple_of(at - j * half, TILE), TILE), unit)
                temp[:, cols] = value
                return functools.reduce(jnp.maximum, fold(jnp.abs(value)), top)

            top = tiles(j * half, (j + 1) * half, passing, jnp.zeros((ROWS, LANES), F32))
            top = tiles((1 - j) * half, (2 - j) * half, plain, top)
            power = exponent(jnp.max(top, axis=1, keepdims=True))
            by = jnp.exp2(-power) * UNIT

            def second(at, carry):
                cols = pl.ds(at, TILE)
                q2s[k, j, :, cols] = code(temp[:, cols], by)
                return carry

            tiles(0, width, second, 0)
            q2s[k, j, :, pl.ds(width, LANES)] = jnp.broadcast_to(power, (ROWS, LANES)).astype(jnp.int32).astype(jnp.int16)
            send((k, "q2", j), q2s.at[k, j], q2r.at[k, j], at_x(step))

    def stage_l(k):
        if k == 0:
            refs_load.wait()
        units = []
        for j in range(2):
            arrive((k, "q2", j), q2r.at[k, j])
            units.append(unit_of(q2r.at[k, j], width))

        def first(at, carry):
            top, qtop = carry
            cols = pl.ds(at, TILE)
            value = local_sum(k, x, cols)
            for j in range(2):
                value += decode(q2r.at[k, j], cols, units[j])
            zbuf[k, :, cols] = value
            top = functools.reduce(jnp.maximum, fold(value), top)
            qtop = functools.reduce(jnp.maximum, fold(own_rows(refs, k, cols)), qtop)
            return (top, qtop)

        low = jnp.full((ROWS, LANES), -jnp.inf, F32)
        top, qtop = tiles(0, width, first, (low, low))
        top = jnp.max(top, axis=1, keepdims=True)
        qtop = jnp.max(qtop, axis=1, keepdims=True)

        def second(at, carry):
            cols = pl.ds(at, TILE)
            value = zbuf[k, :, cols]
            ref = own_rows(refs, k, cols)
            expo = jnp.exp(value - top)
            adds = (expo, expo * value, expo * ref, jnp.exp(ref - qtop))
            return tuple(sum(fold(a), c) for a, c in zip(adds, carry))

        sums = tiles(0, width, second, (jnp.zeros((ROWS, LANES), F32),) * 4)
        total, sum_z, sum_r, qtotal = (jnp.sum(s, axis=1, keepdims=True) for s in sums)
        stat_s[k, 0] = spread((top, total, sum_z, sum_r, qtop, qtotal))
        for d in (1, 3, 2):
            send((k, "sy", d), stat_s.at[k, 0], stat_r.at[k, 0, d - 1], at_y(d))

    def stage_s(k):
        arrive((k, "sy"), stat_r.at[k, 0])
        stat_s[k, 1] = spread(merge([stat_s[k, 0]] + [stat_r[k, 0, d] for d in range(3)]))
        for d in (1, 3, 2):
            send((k, "sz", d), stat_s.at[k, 1], stat_r.at[k, 1, d - 1], at_z(d))

    def stage_t(k):
        c, low = k // SUBS, k % SUBS
        arrive((k, "sz"), stat_r.at[k, 1])
        top, total, sum_z, sum_r, qtop, qtotal = merge([stat_s[k, 1]] + [stat_r[k, 1, d] for d in range(3)])
        lse = top + jnp.log(total)
        qlse = qtop + jnp.log(qtotal)
        mean_z = sum_z / total
        mean_r = sum_r / total
        kl_term = mean_z - mean_r - lse + qlse
        entropy = lse - mean_z
        one = pl.ds(0, LANES)
        adv = own_rows(adv_c, k, one)[:, 0:1]
        weight = own_rows(wgt_c, k, one)[:, 0:1]
        base = adv + 0.04 * (qlse - lse - kl_term) + 0.02 * (entropy - lse)
        picked = weight * adv
        spot = own_rows(tok_c, k, one)[:, 0:1].astype(jnp.int32) - shard * width

        def body(at, carry):
            cols = pl.ds(at, TILE)
            value = zbuf[k, :, cols]
            ref = own_rows(refs, k, cols)
            grad = (weight * jnp.exp(value - lse)) * (base + 0.06 * value - 0.04 * ref)
            here = lax.broadcasted_iota(jnp.int32, (ROWS, TILE), 1) + at
            grad = grad - jnp.where(here == spot, picked, 0.0)
            dl[c, core, x, low, :, cols] = grad.astype(jnp.bfloat16)
            return carry

        spans = [pl.ds(0, half), pl.ds(half, half)]
        tiles(0, half, body, 0)
        mine = dl.at[c, core, x, low, :, spans[0]]
        send((k, "a+", 0), mine, mine, at_x(1))
        tiles(half, width, body, 0)
        mine = dl.at[c, core, x, low, :, spans[1]]
        send((k, "a-", 1), mine, mine, at_x(-1))
        send((k, "a+", 1), mine, mine, at_x(1))
        mine = dl.at[c, core, x, low, :, spans[0]]
        send((k, "a-", 0), mine, mine, at_x(-1))
        send((k, "c", 0), dl.at[c, core, x, low], dl.at[c, core, x, low], at_core())

    def stage_f(k):
        c, low = k // SUBS, k % SUBS
        left = dl.at[c, core, xof(-1), low, :, pl.ds(0, half)]
        arrive((k, "a+", 0), left)
        send((k, "a", 1), left, left, at_x(1))
        right = dl.at[c, core, xof(1), low, :, pl.ds(half, half)]
        arrive((k, "a-", 1), right)
        send((k, "a", -1), right, right, at_x(-1))

    def stage_c(k):
        c, low = k // SUBS, k % SUBS
        arrive((k, "a+", 1), dl.at[c, core, xof(-1), low, :, pl.ds(half, half)])
        send((k, "c", 1), dl.at[c, core, xof(-1), low], dl.at[c, core, xof(-1), low], at_core())
        arrive((k, "a-", 0), dl.at[c, core, xof(1), low, :, pl.ds(0, half)])
        send((k, "c", 3), dl.at[c, core, xof(1), low], dl.at[c, core, xof(1), low], at_core())
        arrive((k, "a", 1), dl.at[c, core, xof(2), low, :, pl.ds(0, half)])
        arrive((k, "a", -1), dl.at[c, core, xof(2), low, :, pl.ds(half, half)])
        send((k, "c", 2), dl.at[c, core, xof(2), low], dl.at[c, core, xof(2), low], at_core())

    def stage_p(k):
        arrive((SUBS * k, "c"), dl.at[k, 1 - core])
        bring(dl.at[k], dl_out.at[k])

        def step(i, carry):
            at = pl.ds(pl.multiple_of(i * PTILE, PTILE), PTILE)
            rows = dl[k].reshape(16 * ROWS, width)
            out = lax.dot_general(rows, head[at, :], (((1,), (1,)), ((), ())), preferred_element_type=F32)
            pg[k, :, :, :, :, at] = out.reshape(2, NZ, 2, ROWS, PTILE)
            return carry

        lax.fori_loop(0, dhalf // PTILE, step, 0)
        for d in (1, 3, 2):
            yy = yof(d)
            src = pg.at[k, lax.div(yy, 2), :, lax.rem(yy, 2), :, cols0]
            send((k, "g1y", d), src, ra.at[k, 0, d - 1], at_y(d))
        lax.fori_loop(dhalf // PTILE, depth // PTILE, step, 0)
        for d in (1, 3, 2):
            src = pg.at[k, :, zof(d), :, :, cols1]
            send((k, "g1z", d), src, rb.at[k, 0, d - 1], at_z(d))

    def stage_u(k):
        arrive((k, "g1y"), ra.at[k, 0])
        value = pg[k, ycd, :, ylo, :, cols0]
        for d in range(3):
            value += ra[k, 0, d]
        rsum[k, 0] = value
        for d in (1, 3, 2):
            send((k, "g2z", d), rsum.at[k, 0, zof(d)], ra.at[k, 1, d - 1, 0], at_z(d))
        arrive((k, "g1z"), rb.at[k, 0])
        value = pg[k, :, z, :, :, cols1]
        for d in range(3):
            value += rb[k, 0, d]
        rsum[k, 1] = value.reshape(4, ROWS, dhalf)
        for d in (1, 3, 2):
            send((k, "g2y", d), rsum.at[k, 1, yof(d)], ra.at[k, 1, d - 1, 1], at_y(d))

    def stage_v(k):
        rows = pl.ds(ROWS * k, ROWS)
        for j, (name, mine) in enumerate((("g2z", z), ("g2y", y))):
            value = rsum[k, j, mine]
            arrive((k, name), ra.at[k, 1, :, j])
            for d in range(3):
                value += ra[k, 1, d, j]
            hgrad_ref[rows, pl.ds(j * dhalf, dhalf)] = value

    stages = dict(
        A=stage_a, B=stage_b, M=stage_m, Q=stage_q, R=stage_r, L=stage_l, S=stage_s, T=stage_t,
        F=stage_f, C=stage_c, P=stage_p, U=stage_u, V=stage_v,
    )
    for word in ORDER:
        with jax.named_scope("stage_" + word):
            stages[word[0]](int(word[1:]))
    three = pl.ds(0, 3)
    for name, view in (
        ("core0", part.at[0, 1 - core]), ("core1", part.at[1, 1 - core]),
        ("h1", dl.at[0, 0, three, 0]), ("h2", dl.at[three, 0, :, 0]),
        ("q1", q1s), ("q2", q2s), ("s", stat_r), ("g1y", ra.at[:, 0]), ("g1z", rb), ("g2", ra.at[:, 1, :, pl.ds(0, 2)]),
        ("c", dl.at[:, 1 - core]), ("a", dl.at[:, core, three]),
    ):
        sent(name, view)
    for copy in locals_[len(own) + len(head_loads) + 1 :]:
        copy.wait()


def per_device(hidden, head, ref_logits, token_ids, group_ids, response_mask, advantages):
    depth, width = head.shape
    groups = advantages.shape[0]
    dhalf = depth // 2
    bf16, i16 = jnp.bfloat16, jnp.int16
    any_space = pl.BlockSpec(memory_space=pl.ANY)
    in_vmem = pl.BlockSpec(memory_space=pltpu.VMEM)
    hidden_grad, grads, rows = pl.pallas_call(
        kernel,
        out_shape=(
            jax.ShapeDtypeStruct((CHUNKS * ROWS, depth), F32),
            jax.ShapeDtypeStruct((CHUNKS, 2, NX, SUBS, ROWS, width), bf16),
            jax.ShapeDtypeStruct((CHUNKS, 2, NZ, 2, ROWS, depth), bf16),
        ),
        in_specs=[any_space] * 3 + [in_vmem] * 4,
        out_specs=(in_vmem, any_space, any_space),
        scratch_shapes=[
            pltpu.VMEM((depth, width), bf16),
            pltpu.VMEM((CHUNKS, 2, NZ, 2, ROWS, depth), bf16),
            pltpu.VMEM(ref_logits.shape, bf16),
            pltpu.VMEM((2, 2, NX, SUBS, ROWS, width), F32),
            pltpu.VMEM((CHUNKS, NX, SUBS, ROWS, width), F32),
            pltpu.VMEM((ROWS, width), F32),
            pltpu.VMEM((SUBS * CHUNKS, 2, ROWS, width // 2 + LANES), i16),
            pltpu.VMEM((SUBS * CHUNKS, 2, ROWS, width // 2 + LANES), i16),
            pltpu.VMEM((SUBS * CHUNKS, 2, ROWS, width + LANES), i16),
            pltpu.VMEM((SUBS * CHUNKS, 2, ROWS, width + LANES), i16),
            pltpu.VMEM((SUBS * CHUNKS, ROWS, width), F32),
            pltpu.VMEM((SUBS * CHUNKS, 2, ROWS, LANES), F32),
            pltpu.VMEM((SUBS * CHUNKS, 2, 3, ROWS, LANES), F32),
            pltpu.VMEM((CHUNKS, 2, NX, SUBS, ROWS, width), bf16),
            pltpu.VMEM((CHUNKS, 2, NZ, 2, ROWS, depth), F32),
            pltpu.VMEM((CHUNKS, 2, 3, 4, ROWS, dhalf), F32),
            pltpu.VMEM((CHUNKS, 2, 4, ROWS, dhalf), F32),
            pltpu.VMEM((CHUNKS, 1, 3, 2, 2, ROWS, dhalf), F32),
            pltpu.VMEM((LANES, LANES), F32),
            pltpu.VMEM((LANES, LANES), F32),
            pltpu.VMEM((LANES, LANES), F32),
            pltpu.SemaphoreType.DMA((len(SENDERS),)),
            pltpu.SemaphoreType.DMA((34 * CHUNKS,)),
            pltpu.SemaphoreType.DMA((20,)),
        ],
        compiler_params=pltpu.CompilerParams(
            collective_id=0, has_side_effects=True, vmem_limit_bytes=62 * 1024 * 1024
        ),
    )(
        hidden, head, ref_logits,
        token_ids.reshape(8, LANES), group_ids.reshape(8, LANES), response_mask.reshape(8, LANES),
        advantages.reshape(1, groups),
    )
    head_grad = lax.dot_general(
        rows.reshape(-1, depth), grads.reshape(-1, width), (((0,), (0,)), ((), ())), preferred_element_type=F32
    )
    return (hidden_grad, head_grad)


def solution(mesh):
    placed = (
        P("vocab", ("dp", "rows")),
        P(("dp", "rows"), "vocab"),
        P(("dp", "rows"), "vocab"),
        P(),
        P(),
        P(),
        P(),
    )
    return jax.shard_map(
        per_device,
        mesh=mesh,
        in_specs=placed,
        out_specs=(P("vocab", ("dp", "rows")), P(("dp", "rows"), "vocab")),
        check_vma=False,
    )
```

```python
import functools

import jax
import jax.numpy as jnp
from jax import lax
from jax.experimental import pallas as pl
from jax.experimental.pallas import tpu as pltpu
from jax.sharding import PartitionSpec as P

MESH = pl.DeviceIdType.MESH
CHUNKS = 4
NX = 4
NY = 4
NZ = 4
ROWS = 16
SUBS = 2
TILE = 2048
MTILE = 1024
PTILE = 512
LANES = 128
UNIT = 32000.0
F32 = jnp.float32
SPANS = (512, 1024, 1024, 1024, 512)
SENDERS = ("core0", "core1", "h1", "h2", "q1", "q2", "s", "g1y", "g1z", "g2", "c", "a")

ORDER = (
    "A0", "B0", "A1", "B1", "M0", "Q0", "M1", "A2", "Q1", "R0", "B2", "R1", "A3", "Q2", "L0", "B3", "Q3",
    "R2", "S0", "L1", "R3", "M2", "T0", "S1", "L2", "Q4", "F0", "T1", "Q5", "L3", "R4", "M3", "S2", "S3",
    "F1", "Q6", "T2", "L4", "R5", "Q7", "C0", "C1", "R6", "S4", "P0", "T3", "L5", "F2", "R7", "L6", "S5",
    "F3", "T4", "S6", "T5", "C2", "L7", "T6", "C3", "U0", "S7", "F4", "P1", "F5", "T7", "V0", "C4", "C5",
    "F6", "U1", "F7", "P2", "C6", "C7", "P3", "U2", "V1", "U3", "V2", "V3",
)


def fold(values):
    return [values[:, j : j + LANES] for j in range(0, values.shape[1], LANES)]


def column(row):
    square = (LANES, LANES)
    same = lax.broadcasted_iota(jnp.int32, square, 0) == lax.broadcasted_iota(jnp.int32, square, 1)
    return jnp.sum(jnp.where(same, jnp.broadcast_to(row, square), 0.0), axis=1, keepdims=True)


def spread(columns):
    rows = columns[0].shape[0]
    lane = lax.broadcasted_iota(jnp.int32, (rows, LANES), 1)
    tile = jnp.zeros((rows, LANES), F32)
    for j, value in enumerate(columns):
        tile = jnp.where(lane == j, value, tile)
    return tile


def merge(tiles):
    get = lambda tile, j: tile[:, j : j + 1]
    top = functools.reduce(jnp.maximum, [get(t, 0) for t in tiles])
    qtop = functools.reduce(jnp.maximum, [get(t, 4) for t in tiles])
    scale = [jnp.exp(get(t, 0) - top) for t in tiles]
    qscale = [jnp.exp(get(t, 4) - qtop) for t in tiles]
    total, sum_z, sum_r = (sum(get(t, j) * s for t, s in zip(tiles, scale)) for j in (1, 2, 3))
    qtotal = sum(get(t, 5) * s for t, s in zip(tiles, qscale))
    return (top, total, sum_z, sum_r, qtop, qtotal)


def kernel(
    hidden_ref, head_ref, refs_ref, token_ref, group_ref, mask_ref, adv_ref,
    hgrad_ref, dl_out, hid_out,
    head, hid, refs, part, crecv, temp, q1s, q1r, q2s, q2r, zbuf, stat_s, stat_r, dl, pg, pgs, ga, gb, gc, rsum,
    tok_c, adv_c, wgt_c, hid_t, send_sem, recv_sem, local_sem,
):
    x = lax.axis_index("dp")
    core = lax.axis_index("rows")
    shard = lax.axis_index("vocab")
    y, z = lax.rem(shard, NY), lax.div(shard, NY)
    width = head.shape[1]
    half = width // 2
    depth = head.shape[0]
    dhalf = depth // 2
    block = 2 * x + core
    ycd, ylo = lax.div(y, 2), lax.rem(y, 2)

    def xof(step):
        return lax.rem(x + step + 2 * NX, NX)

    def yof(step):
        return lax.rem(y + step, NY)

    def zof(step):
        return lax.rem(z + step, NZ)

    def at_core():
        return {"rows": 1 - core}

    def at_x(step):
        return {"dp": xof(step)}

    def at_y(step):
        return {"vocab": z * NY + yof(step)}

    def at_z(step):
        return {"vocab": zof(step) * NY + y}

    numbers = {}

    def number(key):
        if key[1] in ("q1", "q2", "a+", "a-", "a"):
            return numbers.setdefault(key, len(numbers))
        if key[1] == "c":
            return numbers.setdefault((key[0] // SUBS, "c"), len(numbers))
        return numbers.setdefault(key[:2], len(numbers))

    def send(key, src, dst, device):
        name = key[1] + str(key[0] // SUBS % 2) if key[1] == "core" else key[1]
        n = next(i for i, start in enumerate(SENDERS) if name.startswith(start))
        pltpu.make_async_remote_copy(
            src_ref=src, dst_ref=dst, send_sem=send_sem.at[n], recv_sem=recv_sem.at[number(key)],
            device_id=device, device_id_type=MESH,
        ).start()

    def arrive(key, view):
        pltpu.make_async_copy(view, view, recv_sem.at[number(key)]).wait()

    def sent(name, view):
        pltpu.make_async_copy(view, view, send_sem.at[SENDERS.index(name)]).wait()

    locals_ = []

    def bring(src, dst):
        copy = pltpu.make_async_copy(src, dst, local_sem.at[len(locals_)])
        copy.start()
        locals_.append(copy)
        return copy

    own = [bring(hidden_ref.at[pl.ds(ROWS * k, ROWS)], hid.at[k, ycd, z, ylo]) for k in range(CHUNKS)]
    head_loads = [
        bring(head_ref.at[pl.ds(j * depth // 4, depth // 4)], head.at[pl.ds(j * depth // 4, depth // 4)])
        for j in range(4)
    ]
    refs_load = bring(refs_ref, refs)
    barrier = pltpu.get_barrier_semaphore()
    peers = [at_core(), at_x(1), at_x(-1)] + [at_y(d) for d in (1, 2, 3)] + [at_z(d) for d in (1, 2, 3)]
    for peer in peers:
        pl.semaphore_signal(barrier, inc=1, device_id=peer, device_id_type=MESH)
    pl.semaphore_wait(barrier, len(peers))

    cols0, cols1 = pl.ds(0, dhalf), pl.ds(dhalf, dhalf)
    def own_row(ref):
        values = ref[...].astype(F32)
        at = lax.broadcasted_iota(jnp.int32, values.shape, 0) == block
        return jnp.sum(jnp.where(at, values, 0.0), axis=0, keepdims=True)

    groups = adv_ref.shape[1]
    group_col = column(own_row(group_ref))
    group_at = lax.broadcasted_iota(jnp.int32, (LANES, groups), 1).astype(F32)
    adv_col = jnp.sum(jnp.where(group_col == group_at, adv_ref[...], 0.0), axis=1, keepdims=True)
    tok_c[...] = jnp.broadcast_to(column(own_row(token_ref)), tok_c.shape)
    adv_c[...] = jnp.broadcast_to(adv_col, adv_c.shape)
    wgt_c[...] = jnp.broadcast_to(column(own_row(mask_ref)), wgt_c.shape)

    def own_rows(ref, k, cols):
        at = 4 * ROWS * (k % SUBS) + ROWS * (k // SUBS)
        return ref[pl.ds(at, ROWS), cols].astype(F32)

    def tiles(lo, hi, body, init):
        def step(i, carry):
            return body(pl.multiple_of(i * TILE, TILE), carry)

        return lax.fori_loop(lo // TILE, hi // TILE, step, init)

    def exponent(top):
        return jnp.floor(jnp.log2(jnp.maximum(top, 1e-30))) + 1.0

    def code(values, by):
        return jnp.round(values * by).astype(jnp.int32).astype(jnp.int16)

    def decode(ref, cols, by):
        return ref[:, cols].astype(jnp.int32).astype(F32) * by

    def unit_of(ref, at):
        return jnp.exp2(ref[:, pl.ds(at, LANES)].astype(jnp.int32).astype(F32)[:, 0:1]) * (1.0 / UNIT)

    def local_sum(k, xd, cols):
        c, low = k // SUBS, k % SUBS
        return part[c % 2, core, xd, low, :, cols] + crecv[c, xd, low, :, cols]

    def stage_a(k):
        own[k].wait()
        for d in (1, 3, 2):
            mine = hid.at[k, ycd, z, ylo, :, cols0]
            send((k, "h1y", d), mine, mine, at_y(d))
            mine = hid.at[k, ycd, z, ylo, :, cols1]
            send((k, "h1z", d), mine, mine, at_z(d))

    def stage_b(k):
        arrive((k, "h1y"), dl.at[0, 0, pl.ds(0, 3), 0, :, cols0])
        arrive((k, "h1z"), dl.at[0, 0, pl.ds(0, 3), 0, :, cols0])
        for d in (1, 3, 2):
            mine = hid.at[k, :, z, :, :, cols0]
            send((k, "h2z", d), mine, mine, at_z(d))
            mine = hid.at[k, ycd, :, ylo, :, cols1]
            send((k, "h2y", d), mine, mine, at_y(d))

    def stage_m(k):
        if k == 0:
            for copy in head_loads:
                copy.wait()
        arrive((k, "h2z"), dl.at[0, :, pl.ds(0, 3), :, :, cols0])
        arrive((k, "h2y"), dl.at[0, :, pl.ds(0, 3), :, :, cols0])
        slot = k % 2
        hid_t[:, pl.ds(16 * ROWS * k, 16 * ROWS)] = jnp.swapaxes(hid[k].reshape(16 * ROWS, depth), 0, 1)
        if k == CHUNKS - 1:
            bring(hid_t, hid_out)
        if k >= 2:
            sent("core" + str(slot), part.at[slot, 1 - core])
        for lows in ((0,), (1,)) if k == 0 else ((0, 1),):
            low, many = pl.ds(lows[0], len(lows)), len(lows)
            for g in range(width // MTILE):
                cols = pl.ds(g * MTILE, MTILE)
                rows = hid[k, :, :, low].reshape(8 * many * ROWS, depth)
                out = jnp.dot(rows, head[:, cols], preferred_element_type=F32)
                part[slot, :, :, low, :, cols] = out.reshape(2, NX, many, ROWS, MTILE)
                src = part.at[slot, 1 - core, :, low, :, cols]
                send((SUBS * k + lows[0], "core", g), src, crecv.at[k, :, low, :, cols], at_core())

    def stage_q(k):
        if k < SUBS:
            arrive((k, "core"), crecv.at[0, :, k])
        elif k % SUBS == 0:
            arrive((k, "core"), crecv.at[k // SUBS])
        xd = xof(2)

        def first(at, top):
            cols = pl.ds(at, TILE)
            value = local_sum(k, xd, cols)
            temp[:, cols] = value
            return functools.reduce(jnp.maximum, fold(jnp.abs(value)), top)

        top = tiles(0, width, first, jnp.zeros((ROWS, LANES), F32))
        power = exponent(jnp.max(top, axis=1, keepdims=True))
        by = jnp.exp2(-power) * UNIT
        for j in range(2):

            def second(at, carry):
                q1s[k, j, :, pl.ds(pl.multiple_of(at - j * half, TILE), TILE)] = code(temp[:, pl.ds(at, TILE)], by)
                return carry

            tiles(j * half, (j + 1) * half, second, 0)
            q1s[k, j, :, pl.ds(half, LANES)] = jnp.broadcast_to(power, (ROWS, LANES)).astype(jnp.int32).astype(jnp.int16)
            send((k, "q1", j), q1s.at[k, j], q1r.at[k, j], at_x(1 if j == 0 else -1))

    def stage_r(k):
        for j in range(2):
            step = 1 if j == 0 else -1
            xd = xof(step)
            arrive((k, "q1", j), q1r.at[k, j])
            unit = unit_of(q1r.at[k, j], half)

            def plain(at, top):
                cols = pl.ds(at, TILE)
                value = local_sum(k, xd, cols)
                temp[:, cols] = value
                return functools.reduce(jnp.maximum, fold(jnp.abs(value)), top)

            def passing(at, top):
                cols = pl.ds(at, TILE)
                value = local_sum(k, xd, cols)
                value += decode(q1r.at[k, j], pl.ds(pl.multiple_of(at - j * half, TILE), TILE), unit)
                temp[:, cols] = value
                return functools.reduce(jnp.maximum, fold(jnp.abs(value)), top)

            top = tiles(j * half, (j + 1) * half, passing, jnp.zeros((ROWS, LANES), F32))
            top = tiles((1 - j) * half, (2 - j) * half, plain, top)
            power = exponent(jnp.max(top, axis=1, keepdims=True))
            by = jnp.exp2(-power) * UNIT

            def second(at, carry):
                cols = pl.ds(at, TILE)
                q2s[k, j, :, cols] = code(temp[:, cols], by)
                return carry

            tiles(0, width, second, 0)
            q2s[k, j, :, pl.ds(width, LANES)] = jnp.broadcast_to(power, (ROWS, LANES)).astype(jnp.int32).astype(jnp.int16)
            send((k, "q2", j), q2s.at[k, j], q2r.at[k, j], at_x(step))

    def stage_l(k):
        if k == 0:
            refs_load.wait()
        units = []
        for j in range(2):
            arrive((k, "q2", j), q2r.at[k, j])
            units.append(unit_of(q2r.at[k, j], width))

        def first(at, carry):
            top, qtop = carry
            cols = pl.ds(at, TILE)
            value = local_sum(k, x, cols)
            for j in range(2):
                value += decode(q2r.at[k, j], cols, units[j])
            zbuf[k, :, cols] = value
            top = functools.reduce(jnp.maximum, fold(value), top)
            qtop = functools.reduce(jnp.maximum, fold(own_rows(refs, k, cols)), qtop)
            return (top, qtop)

        low = jnp.full((ROWS, LANES), -jnp.inf, F32)
        top, qtop = tiles(0, width, first, (low, low))
        top = jnp.max(top, axis=1, keepdims=True)
        qtop = jnp.max(qtop, axis=1, keepdims=True)

        def second(at, carry):
            cols = pl.ds(at, TILE)
            value = zbuf[k, :, cols]
            ref = own_rows(refs, k, cols)
            expo = jnp.exp(value - top)
            adds = (expo, expo * value, expo * ref, jnp.exp(ref - qtop))
            return tuple(sum(fold(a), c) for a, c in zip(adds, carry))

        sums = tiles(0, width, second, (jnp.zeros((ROWS, LANES), F32),) * 4)
        total, sum_z, sum_r, qtotal = (jnp.sum(s, axis=1, keepdims=True) for s in sums)
        stat_s[k, 0] = spread((top, total, sum_z, sum_r, qtop, qtotal))
        for d in (1, 3, 2):
            send((k, "sy", d), stat_s.at[k, 0], stat_r.at[k, 0, d - 1], at_y(d))

    def stage_s(k):
        arrive((k, "sy"), stat_r.at[k, 0])
        stat_s[k, 1] = spread(merge([stat_s[k, 0]] + [stat_r[k, 0, d] for d in range(3)]))
        for d in (1, 3, 2):
            send((k, "sz", d), stat_s.at[k, 1], stat_r.at[k, 1, d - 1], at_z(d))

    def stage_t(k):
        c, low = k // SUBS, k % SUBS
        arrive((k, "sz"), stat_r.at[k, 1])
        top, total, sum_z, sum_r, qtop, qtotal = merge([stat_s[k, 1]] + [stat_r[k, 1, d] for d in range(3)])
        lse = top + jnp.log(total)
        qlse = qtop + jnp.log(qtotal)
        mean_z = sum_z / total
        mean_r = sum_r / total
        kl_term = mean_z - mean_r - lse + qlse
        entropy = lse - mean_z
        one = pl.ds(0, LANES)
        adv = own_rows(adv_c, k, one)[:, 0:1]
        weight = own_rows(wgt_c, k, one)[:, 0:1]
        base = adv + 0.04 * (qlse - lse - kl_term) + 0.02 * (entropy - lse)
        picked = weight * adv
        spot = own_rows(tok_c, k, one)[:, 0:1].astype(jnp.int32) - shard * width

        def body(at, carry):
            cols = pl.ds(at, TILE)
            value = zbuf[k, :, cols]
            ref = own_rows(refs, k, cols)
            grad = (weight * jnp.exp(value - lse)) * (base + 0.06 * value - 0.04 * ref)
            here = lax.broadcasted_iota(jnp.int32, (ROWS, TILE), 1) + at
            grad = grad - jnp.where(here == spot, picked, 0.0)
            dl[c, core, x, low, :, cols] = grad.astype(jnp.bfloat16)
            return carry

        spans = [pl.ds(0, half), pl.ds(half, half)]
        tiles(0, half, body, 0)
        mine = dl.at[c, core, x, low, :, spans[0]]
        send((k, "a+", 0), mine, mine, at_x(1))
        tiles(half, width, body, 0)
        mine = dl.at[c, core, x, low, :, spans[1]]
        send((k, "a-", 1), mine, mine, at_x(-1))
        send((k, "a+", 1), mine, mine, at_x(1))
        mine = dl.at[c, core, x, low, :, spans[0]]
        send((k, "a-", 0), mine, mine, at_x(-1))
        send((k, "c", 0), dl.at[c, core, x, low], dl.at[c, core, x, low], at_core())

    def stage_f(k):
        c, low = k // SUBS, k % SUBS
        left = dl.at[c, core, xof(-1), low, :, pl.ds(0, half)]
        arrive((k, "a+", 0), left)
        send((k, "a", 1), left, left, at_x(1))
        right = dl.at[c, core, xof(1), low, :, pl.ds(half, half)]
        arrive((k, "a-", 1), right)
        send((k, "a", -1), right, right, at_x(-1))

    def stage_c(k):
        c, low = k // SUBS, k % SUBS
        arrive((k, "a+", 1), dl.at[c, core, xof(-1), low, :, pl.ds(half, half)])
        send((k, "c", 1), dl.at[c, core, xof(-1), low], dl.at[c, core, xof(-1), low], at_core())
        arrive((k, "a-", 0), dl.at[c, core, xof(1), low, :, pl.ds(0, half)])
        send((k, "c", 3), dl.at[c, core, xof(1), low], dl.at[c, core, xof(1), low], at_core())
        arrive((k, "a", 1), dl.at[c, core, xof(2), low, :, pl.ds(0, half)])
        arrive((k, "a", -1), dl.at[c, core, xof(2), low, :, pl.ds(half, half)])
        send((k, "c", 2), dl.at[c, core, xof(2), low], dl.at[c, core, xof(2), low], at_core())

    def stage_p(k):
        arrive((SUBS * k, "c"), dl.at[k, 1 - core])
        bring(dl.at[k], dl_out.at[k])

        def step(i, carry):
            at = pl.ds(pl.multiple_of(i * PTILE, PTILE), PTILE)
            rows = dl[k].reshape(16 * ROWS, width)
            out = lax.dot_general(rows, head[at, :], (((1,), (1,)), ((), ())), preferred_element_type=F32)
            pg[k, :, :, :, :, at] = out.reshape(2, NZ, 2, ROWS, PTILE)
            pgs[k, :, :, :, :, at] = out.astype(jnp.bfloat16).reshape(2, NZ, 2, ROWS, PTILE)
            return carry

        lax.fori_loop(0, dhalf // PTILE, step, 0)
        for d in (1, 3, 2):
            yy = yof(d)
            src = pgs.at[k, lax.div(yy, 2), :, lax.rem(yy, 2), :, cols0]
            send((k, "g1y", d), src, ga.at[k, d - 1], at_y(d))
        lax.fori_loop(dhalf // PTILE, depth // PTILE, step, 0)
        for d in (1, 3, 2):
            src = pgs.at[k, :, zof(d), :, :, cols1]
            send((k, "g1z", d), src, gb.at[k, d - 1], at_z(d))

    def stage_u(k):
        arrive((k, "g1y"), ga.at[k])
        value = pg[k, ycd, :, ylo, :, cols0]
        for d in range(3):
            value += ga[k, d].astype(F32)
        rsum[k, 0] = value
        for d in (1, 3, 2):
            send((k, "g2z", d), rsum.at[k, 0, zof(d)], gc.at[k, d - 1, 0], at_z(d))
        arrive((k, "g1z"), gb.at[k])
        value = pg[k, :, z, :, :, cols1]
        for d in range(3):
            value += gb[k, d].astype(F32)
        rsum[k, 1] = value.reshape(4, ROWS, dhalf)
        for d in (1, 3, 2):
            send((k, "g2y", d), rsum.at[k, 1, yof(d)], gc.at[k, d - 1, 1], at_y(d))

    def stage_v(k):
        rows = pl.ds(ROWS * k, ROWS)
        for j, (name, mine) in enumerate((("g2z", z), ("g2y", y))):
            value = rsum[k, j, mine]
            arrive((k, name), gc.at[k, :, j])
            for d in range(3):
                value += gc[k, d, j]
            hgrad_ref[rows, pl.ds(j * dhalf, dhalf)] = value

    stages = dict(
        A=stage_a, B=stage_b, M=stage_m, Q=stage_q, R=stage_r, L=stage_l, S=stage_s, T=stage_t,
        F=stage_f, C=stage_c, P=stage_p, U=stage_u, V=stage_v,
    )
    for word in ORDER:
        with jax.named_scope("stage_" + word):
            stages[word[0]](int(word[1:]))
    three = pl.ds(0, 3)
    for name, view in (
        ("core0", part.at[0, 1 - core]), ("core1", part.at[1, 1 - core]),
        ("h1", dl.at[0, 0, three, 0]), ("h2", dl.at[three, 0, :, 0]),
        ("q1", q1s), ("q2", q2s), ("s", stat_r), ("g1y", ga), ("g1z", gb), ("g2", gc),
        ("c", dl.at[:, 1 - core]), ("a", dl.at[:, core, three]),
    ):
        sent(name, view)
    for copy in locals_[len(own) + len(head_loads) + 1 :]:
        copy.wait()


def head_kernel(rows_ref, grads_ref, out_ref, rows, grads, outs, row_sem, in_sem, out_sem):
    starts = [sum(SPANS[:i]) for i in range(len(SPANS))]
    spans = [pl.ds(at, size) for at, size in zip(starts, SPANS)]
    loads = [pltpu.make_async_copy(rows_ref, rows, row_sem.at[0])]
    loads += [
        pltpu.make_async_copy(grads_ref.at[:, span], grads.at[:, span], in_sem.at[i]) for i, span in enumerate(spans)
    ]
    loads[0].start()
    loads[1].start()
    loads[2].start()
    loads[0].wait()
    stores = []
    for i, span in enumerate(spans):
        loads[1 + i].wait()
        if i + 3 < len(loads):
            loads[i + 3].start()
        if i >= 2:
            stores[i - 2].wait()
        here = outs.at[i % 2, :, pl.ds(0, SPANS[i])]
        here[...] = jnp.dot(rows[...], grads[:, span], preferred_element_type=F32)
        stores.append(pltpu.make_async_copy(here, out_ref.at[:, span], out_sem.at[i]))
        stores[-1].start()
    stores[-2].wait()
    stores[-1].wait()


def head_gradient(rows, grads):
    (depth, tokens), width = rows.shape, grads.shape[1]
    any_space = pl.BlockSpec(memory_space=pl.ANY)
    return pl.pallas_call(
        head_kernel,
        out_shape=jax.ShapeDtypeStruct((depth, width), F32),
        in_specs=[any_space] * 2,
        out_specs=any_space,
        scratch_shapes=[
            pltpu.VMEM((depth, tokens), rows.dtype),
            pltpu.VMEM((tokens, width), grads.dtype),
            pltpu.VMEM((2, depth, max(SPANS)), F32),
            pltpu.SemaphoreType.DMA((1,)),
            pltpu.SemaphoreType.DMA((len(SPANS),)),
            pltpu.SemaphoreType.DMA((len(SPANS),)),
        ],
        compiler_params=pltpu.CompilerParams(vmem_limit_bytes=56 * 1024 * 1024),
    )(rows, grads)


def per_device(hidden, head, ref_logits, token_ids, group_ids, response_mask, advantages):
    depth, width = head.shape
    groups = advantages.shape[0]
    dhalf = depth // 2
    bf16, i16 = jnp.bfloat16, jnp.int16
    any_space = pl.BlockSpec(memory_space=pl.ANY)
    in_vmem = pl.BlockSpec(memory_space=pltpu.VMEM)
    hidden_grad, grads, rows = pl.pallas_call(
        kernel,
        out_shape=(
            jax.ShapeDtypeStruct((CHUNKS * ROWS, depth), F32),
            jax.ShapeDtypeStruct((CHUNKS, 2, NX, SUBS, ROWS, width), bf16),
            jax.ShapeDtypeStruct((depth, 16 * ROWS * CHUNKS), bf16),
        ),
        in_specs=[any_space] * 3 + [in_vmem] * 4,
        out_specs=(in_vmem, any_space, any_space),
        scratch_shapes=[
            pltpu.VMEM((depth, width), bf16),
            pltpu.VMEM((CHUNKS, 2, NZ, 2, ROWS, depth), bf16),
            pltpu.VMEM(ref_logits.shape, bf16),
            pltpu.VMEM((2, 2, NX, SUBS, ROWS, width), F32),
            pltpu.VMEM((CHUNKS, NX, SUBS, ROWS, width), F32),
            pltpu.VMEM((ROWS, width), F32),
            pltpu.VMEM((SUBS * CHUNKS, 2, ROWS, width // 2 + LANES), i16),
            pltpu.VMEM((SUBS * CHUNKS, 2, ROWS, width // 2 + LANES), i16),
            pltpu.VMEM((SUBS * CHUNKS, 2, ROWS, width + LANES), i16),
            pltpu.VMEM((SUBS * CHUNKS, 2, ROWS, width + LANES), i16),
            pltpu.VMEM((SUBS * CHUNKS, ROWS, width), F32),
            pltpu.VMEM((SUBS * CHUNKS, 2, ROWS, LANES), F32),
            pltpu.VMEM((SUBS * CHUNKS, 2, 3, ROWS, LANES), F32),
            pltpu.VMEM((CHUNKS, 2, NX, SUBS, ROWS, width), bf16),
            pltpu.VMEM((CHUNKS, 2, NZ, 2, ROWS, depth), F32),
            pltpu.VMEM((CHUNKS, 2, NZ, 2, ROWS, depth), bf16),
            pltpu.VMEM((CHUNKS, 3, 4, ROWS, dhalf), bf16),
            pltpu.VMEM((CHUNKS, 3, 2, 2, ROWS, dhalf), bf16),
            pltpu.VMEM((CHUNKS, 3, 2, ROWS, dhalf), F32),
            pltpu.VMEM((CHUNKS, 2, 4, ROWS, dhalf), F32),
            pltpu.VMEM((LANES, LANES), F32),
            pltpu.VMEM((LANES, LANES), F32),
            pltpu.VMEM((LANES, LANES), F32),
            pltpu.VMEM((depth, 16 * ROWS * CHUNKS), bf16),
            pltpu.SemaphoreType.DMA((len(SENDERS),)),
            pltpu.SemaphoreType.DMA((34 * CHUNKS + 1,)),
            pltpu.SemaphoreType.DMA((20,)),
        ],
        compiler_params=pltpu.CompilerParams(
            collective_id=0, has_side_effects=True, vmem_limit_bytes=62 * 1024 * 1024
        ),
    )(
        hidden, head, ref_logits,
        token_ids.reshape(8, LANES), group_ids.reshape(8, LANES), response_mask.reshape(8, LANES),
        advantages.reshape(1, groups),
    )
    head_grad = head_gradient(rows, grads.reshape(-1, width))
    return (hidden_grad, head_grad)


def solution(mesh):
    placed = (
        P("vocab", ("dp", "rows")),
        P(("dp", "rows"), "vocab"),
        P(("dp", "rows"), "vocab"),
        P(),
        P(),
        P(),
        P(),
    )
    return jax.shard_map(
        per_device,
        mesh=mesh,
        in_specs=placed,
        out_specs=(P("vocab", ("dp", "rows")), P(("dp", "rows"), "vocab")),
        check_vma=False,
    )
```

```python
import functools

import jax
import jax.numpy as jnp
from jax import lax
from jax.experimental import pallas as pl
from jax.experimental.pallas import tpu as pltpu
from jax.sharding import PartitionSpec as P

MESH = pl.DeviceIdType.MESH
CHUNKS = 4
NX = 4
NY = 4
NZ = 4
ROWS = 16
SUBS = 2
TILE = 2048
MTILE = 1024
PTILE = 512
LANES = 128
UNIT = 32000.0
F32 = jnp.float32
SPANS = (512, 1024, 1024, 512)
EARLY = 1024
SENDERS = ("core0", "core1", "h1", "h2", "q1", "q2", "s", "g1y", "g1z", "g2", "c", "a")

ORDER = (
    "A0", "B0", "A1", "B1", "M0", "Q0", "M1", "A2", "Q1", "R0", "B2", "R1", "A3", "Q2", "L0", "B3", "Q3",
    "R2", "S0", "L1", "R3", "M2", "T0", "S1", "L2", "Q4", "F0", "T1", "Q5", "L3", "R4", "M3", "S2", "S3",
    "F1", "Q6", "T2", "L4", "R5", "Q7", "C0", "C1", "R6", "S4", "P0", "T3", "L5", "F2", "R7", "L6", "S5",
    "F3", "T4", "S6", "T5", "C2", "L7", "T6", "C3", "U0", "S7", "F4", "P1", "F5", "T7", "V0", "C4", "C5",
    "F6", "U1", "F7", "P2", "C6", "C7", "P3", "H3", "U2", "V1", "U3", "V2", "V3",
)


def fold(values):
    return [values[:, j : j + LANES] for j in range(0, values.shape[1], LANES)]


def column(row):
    square = (LANES, LANES)
    same = lax.broadcasted_iota(jnp.int32, square, 0) == lax.broadcasted_iota(jnp.int32, square, 1)
    return jnp.sum(jnp.where(same, jnp.broadcast_to(row, square), 0.0), axis=1, keepdims=True)


def spread(columns):
    rows = columns[0].shape[0]
    lane = lax.broadcasted_iota(jnp.int32, (rows, LANES), 1)
    tile = jnp.zeros((rows, LANES), F32)
    for j, value in enumerate(columns):
        tile = jnp.where(lane == j, value, tile)
    return tile


def merge(tiles):
    get = lambda tile, j: tile[:, j : j + 1]
    top = functools.reduce(jnp.maximum, [get(t, 0) for t in tiles])
    qtop = functools.reduce(jnp.maximum, [get(t, 4) for t in tiles])
    scale = [jnp.exp(get(t, 0) - top) for t in tiles]
    qscale = [jnp.exp(get(t, 4) - qtop) for t in tiles]
    total, sum_z, sum_r = (sum(get(t, j) * s for t, s in zip(tiles, scale)) for j in (1, 2, 3))
    qtotal = sum(get(t, 5) * s for t, s in zip(tiles, qscale))
    return (top, total, sum_z, sum_r, qtop, qtotal)


def kernel(
    hidden_ref, head_ref, refs_ref, token_ref, group_ref, mask_ref, adv_ref,
    hgrad_ref, dl_out, hid_out, early_out,
    head, hid, refs, part, crecv, temp, q1s, q1r, q2s, q2r, zbuf, stat_s, stat_r, dl, pg, pgs, ga, gb, gc, rsum,
    tok_c, adv_c, wgt_c, hid_t, early, send_sem, recv_sem, local_sem,
):
    x = lax.axis_index("dp")
    core = lax.axis_index("rows")
    shard = lax.axis_index("vocab")
    y, z = lax.rem(shard, NY), lax.div(shard, NY)
    width = head.shape[1]
    half = width // 2
    depth = head.shape[0]
    dhalf = depth // 2
    block = 2 * x + core
    ycd, ylo = lax.div(y, 2), lax.rem(y, 2)

    def xof(step):
        return lax.rem(x + step + 2 * NX, NX)

    def yof(step):
        return lax.rem(y + step, NY)

    def zof(step):
        return lax.rem(z + step, NZ)

    def at_core():
        return {"rows": 1 - core}

    def at_x(step):
        return {"dp": xof(step)}

    def at_y(step):
        return {"vocab": z * NY + yof(step)}

    def at_z(step):
        return {"vocab": zof(step) * NY + y}

    numbers = {}

    def number(key):
        if key[1] in ("q1", "q2", "a+", "a-", "a"):
            return numbers.setdefault(key, len(numbers))
        if key[1] == "c":
            return numbers.setdefault((key[0] // SUBS, "c"), len(numbers))
        return numbers.setdefault(key[:2], len(numbers))

    def send(key, src, dst, device):
        name = key[1] + str(key[0] // SUBS % 2) if key[1] == "core" else key[1]
        n = next(i for i, start in enumerate(SENDERS) if name.startswith(start))
        pltpu.make_async_remote_copy(
            src_ref=src, dst_ref=dst, send_sem=send_sem.at[n], recv_sem=recv_sem.at[number(key)],
            device_id=device, device_id_type=MESH,
        ).start()

    def arrive(key, view):
        pltpu.make_async_copy(view, view, recv_sem.at[number(key)]).wait()

    def sent(name, view):
        pltpu.make_async_copy(view, view, send_sem.at[SENDERS.index(name)]).wait()

    locals_ = []

    def bring(src, dst):
        copy = pltpu.make_async_copy(src, dst, local_sem.at[len(locals_)])
        copy.start()
        locals_.append(copy)
        return copy

    own = [bring(hidden_ref.at[pl.ds(ROWS * k, ROWS)], hid.at[k, ycd, z, ylo]) for k in range(CHUNKS)]
    head_loads = [
        bring(head_ref.at[pl.ds(j * depth // 4, depth // 4)], head.at[pl.ds(j * depth // 4, depth // 4)])
        for j in range(4)
    ]
    refs_load = bring(refs_ref, refs)
    barrier = pltpu.get_barrier_semaphore()
    peers = [at_core(), at_x(1), at_x(-1)] + [at_y(d) for d in (1, 2, 3)] + [at_z(d) for d in (1, 2, 3)]
    for peer in peers:
        pl.semaphore_signal(barrier, inc=1, device_id=peer, device_id_type=MESH)
    pl.semaphore_wait(barrier, len(peers))

    cols0, cols1 = pl.ds(0, dhalf), pl.ds(dhalf, dhalf)
    def own_row(ref):
        values = ref[...].astype(F32)
        at = lax.broadcasted_iota(jnp.int32, values.shape, 0) == block
        return jnp.sum(jnp.where(at, values, 0.0), axis=0, keepdims=True)

    groups = adv_ref.shape[1]
    group_col = column(own_row(group_ref))
    group_at = lax.broadcasted_iota(jnp.int32, (LANES, groups), 1).astype(F32)
    adv_col = jnp.sum(jnp.where(group_col == group_at, adv_ref[...], 0.0), axis=1, keepdims=True)
    tok_c[...] = jnp.broadcast_to(column(own_row(token_ref)), tok_c.shape)
    adv_c[...] = jnp.broadcast_to(adv_col, adv_c.shape)
    wgt_c[...] = jnp.broadcast_to(column(own_row(mask_ref)), wgt_c.shape)

    def own_rows(ref, k, cols):
        at = 4 * ROWS * (k % SUBS) + ROWS * (k // SUBS)
        return ref[pl.ds(at, ROWS), cols].astype(F32)

    def tiles(lo, hi, body, init):
        def step(i, carry):
            return body(pl.multiple_of(i * TILE, TILE), carry)

        return lax.fori_loop(lo // TILE, hi // TILE, step, init)

    def exponent(top):
        return jnp.floor(jnp.log2(jnp.maximum(top, 1e-30))) + 1.0

    def code(values, by):
        return jnp.round(values * by).astype(jnp.int32).astype(jnp.int16)

    def decode(ref, cols, by):
        return ref[:, cols].astype(jnp.int32).astype(F32) * by

    def unit_of(ref, at):
        return jnp.exp2(ref[:, pl.ds(at, LANES)].astype(jnp.int32).astype(F32)[:, 0:1]) * (1.0 / UNIT)

    def local_sum(k, xd, cols):
        c, low = k // SUBS, k % SUBS
        return part[c % 2, core, xd, low, :, cols] + crecv[c, xd, low, :, cols]

    def stage_a(k):
        own[k].wait()
        for d in (1, 3, 2):
            mine = hid.at[k, ycd, z, ylo, :, cols0]
            send((k, "h1y", d), mine, mine, at_y(d))
            mine = hid.at[k, ycd, z, ylo, :, cols1]
            send((k, "h1z", d), mine, mine, at_z(d))

    def stage_b(k):
        arrive((k, "h1y"), dl.at[0, 0, pl.ds(0, 3), 0, :, cols0])
        arrive((k, "h1z"), dl.at[0, 0, pl.ds(0, 3), 0, :, cols0])
        for d in (1, 3, 2):
            mine = hid.at[k, :, z, :, :, cols0]
            send((k, "h2z", d), mine, mine, at_z(d))
            mine = hid.at[k, ycd, :, ylo, :, cols1]
            send((k, "h2y", d), mine, mine, at_y(d))

    def stage_m(k):
        if k == 0:
            for copy in head_loads:
                copy.wait()
        arrive((k, "h2z"), dl.at[0, :, pl.ds(0, 3), :, :, cols0])
        arrive((k, "h2y"), dl.at[0, :, pl.ds(0, 3), :, :, cols0])
        slot = k % 2
        hid_t[:, pl.ds(16 * ROWS * k, 16 * ROWS)] = jnp.swapaxes(hid[k].reshape(16 * ROWS, depth), 0, 1)
        if k == CHUNKS - 1:
            bring(hid_t, hid_out)
        if k >= 2:
            sent("core" + str(slot), part.at[slot, 1 - core])
        for lows in ((0,), (1,)) if k == 0 else ((0, 1),):
            low, many = pl.ds(lows[0], len(lows)), len(lows)
            for g in range(width // MTILE):
                cols = pl.ds(g * MTILE, MTILE)
                rows = hid[k, :, :, low].reshape(8 * many * ROWS, depth)
                out = jnp.dot(rows, head[:, cols], preferred_element_type=F32)
                part[slot, :, :, low, :, cols] = out.reshape(2, NX, many, ROWS, MTILE)
                src = part.at[slot, 1 - core, :, low, :, cols]
                send((SUBS * k + lows[0], "core", g), src, crecv.at[k, :, low, :, cols], at_core())

    def stage_q(k):
        if k < SUBS:
            arrive((k, "core"), crecv.at[0, :, k])
        elif k % SUBS == 0:
            arrive((k, "core"), crecv.at[k // SUBS])
        xd = xof(2)

        def first(at, top):
            cols = pl.ds(at, TILE)
            value = local_sum(k, xd, cols)
            temp[:, cols] = value
            return functools.reduce(jnp.maximum, fold(jnp.abs(value)), top)

        top = tiles(0, width, first, jnp.zeros((ROWS, LANES), F32))
        power = exponent(jnp.max(top, axis=1, keepdims=True))
        by = jnp.exp2(-power) * UNIT
        for j in range(2):

            def second(at, carry):
                q1s[k, j, :, pl.ds(pl.multiple_of(at - j * half, TILE), TILE)] = code(temp[:, pl.ds(at, TILE)], by)
                return carry

            tiles(j * half, (j + 1) * half, second, 0)
            q1s[k, j, :, pl.ds(half, LANES)] = jnp.broadcast_to(power, (ROWS, LANES)).astype(jnp.int32).astype(jnp.int16)
            send((k, "q1", j), q1s.at[k, j], q1r.at[k, j], at_x(1 if j == 0 else -1))

    def stage_r(k):
        for j in range(2):
            step = 1 if j == 0 else -1
            xd = xof(step)
            arrive((k, "q1", j), q1r.at[k, j])
            unit = unit_of(q1r.at[k, j], half)

            def plain(at, top):
                cols = pl.ds(at, TILE)
                value = local_sum(k, xd, cols)
                temp[:, cols] = value
                return functools.reduce(jnp.maximum, fold(jnp.abs(value)), top)

            def passing(at, top):
                cols = pl.ds(at, TILE)
                value = local_sum(k, xd, cols)
                value += decode(q1r.at[k, j], pl.ds(pl.multiple_of(at - j * half, TILE), TILE), unit)
                temp[:, cols] = value
                return functools.reduce(jnp.maximum, fold(jnp.abs(value)), top)

            top = tiles(j * half, (j + 1) * half, passing, jnp.zeros((ROWS, LANES), F32))
            top = tiles((1 - j) * half, (2 - j) * half, plain, top)
            power = exponent(jnp.max(top, axis=1, keepdims=True))
            by = jnp.exp2(-power) * UNIT

            def second(at, carry):
                cols = pl.ds(at, TILE)
                q2s[k, j, :, cols] = code(temp[:, cols], by)
                return carry

            tiles(0, width, second, 0)
            q2s[k, j, :, pl.ds(width, LANES)] = jnp.broadcast_to(power, (ROWS, LANES)).astype(jnp.int32).astype(jnp.int16)
            send((k, "q2", j), q2s.at[k, j], q2r.at[k, j], at_x(step))

    def stage_l(k):
        if k == 0:
            refs_load.wait()
        units = []
        for j in range(2):
            arrive((k, "q2", j), q2r.at[k, j])
            units.append(unit_of(q2r.at[k, j], width))

        def first(at, carry):
            top, qtop = carry
            cols = pl.ds(at, TILE)
            value = local_sum(k, x, cols)
            for j in range(2):
                value += decode(q2r.at[k, j], cols, units[j])
            zbuf[k, :, cols] = value
            top = functools.reduce(jnp.maximum, fold(value), top)
            qtop = functools.reduce(jnp.maximum, fold(own_rows(refs, k, cols)), qtop)
            return (top, qtop)

        low = jnp.full((ROWS, LANES), -jnp.inf, F32)
        top, qtop = tiles(0, width, first, (low, low))
        top = jnp.max(top, axis=1, keepdims=True)
        qtop = jnp.max(qtop, axis=1, keepdims=True)

        def second(at, carry):
            cols = pl.ds(at, TILE)
            value = zbuf[k, :, cols]
            ref = own_rows(refs, k, cols)
            expo = jnp.exp(value - top)
            adds = (expo, expo * value, expo * ref, jnp.exp(ref - qtop))
            return tuple(sum(fold(a), c) for a, c in zip(adds, carry))

        sums = tiles(0, width, second, (jnp.zeros((ROWS, LANES), F32),) * 4)
        total, sum_z, sum_r, qtotal = (jnp.sum(s, axis=1, keepdims=True) for s in sums)
        stat_s[k, 0] = spread((top, total, sum_z, sum_r, qtop, qtotal))
        for d in (1, 3, 2):
            send((k, "sy", d), stat_s.at[k, 0], stat_r.at[k, 0, d - 1], at_y(d))

    def stage_s(k):
        arrive((k, "sy"), stat_r.at[k, 0])
        stat_s[k, 1] = spread(merge([stat_s[k, 0]] + [stat_r[k, 0, d] for d in range(3)]))
        for d in (1, 3, 2):
            send((k, "sz", d), stat_s.at[k, 1], stat_r.at[k, 1, d - 1], at_z(d))

    def stage_t(k):
        c, low = k // SUBS, k % SUBS
        arrive((k, "sz"), stat_r.at[k, 1])
        top, total, sum_z, sum_r, qtop, qtotal = merge([stat_s[k, 1]] + [stat_r[k, 1, d] for d in range(3)])
        lse = top + jnp.log(total)
        qlse = qtop + jnp.log(qtotal)
        mean_z = sum_z / total
        mean_r = sum_r / total
        kl_term = mean_z - mean_r - lse + qlse
        entropy = lse - mean_z
        one = pl.ds(0, LANES)
        adv = own_rows(adv_c, k, one)[:, 0:1]
        weight = own_rows(wgt_c, k, one)[:, 0:1]
        base = adv + 0.04 * (qlse - lse - kl_term) + 0.02 * (entropy - lse)
        picked = weight * adv
        spot = own_rows(tok_c, k, one)[:, 0:1].astype(jnp.int32) - shard * width

        def body(at, carry):
            cols = pl.ds(at, TILE)
            value = zbuf[k, :, cols]
            ref = own_rows(refs, k, cols)
            grad = (weight * jnp.exp(value - lse)) * (base + 0.06 * value - 0.04 * ref)
            here = lax.broadcasted_iota(jnp.int32, (ROWS, TILE), 1) + at
            grad = grad - jnp.where(here == spot, picked, 0.0)
            dl[c, core, x, low, :, cols] = grad.astype(jnp.bfloat16)
            return carry

        spans = [pl.ds(0, half), pl.ds(half, half)]
        tiles(0, half, body, 0)
        mine = dl.at[c, core, x, low, :, spans[0]]
        send((k, "a+", 0), mine, mine, at_x(1))
        tiles(half, width, body, 0)
        mine = dl.at[c, core, x, low, :, spans[1]]
        send((k, "a-", 1), mine, mine, at_x(-1))
        send((k, "a+", 1), mine, mine, at_x(1))
        mine = dl.at[c, core, x, low, :, spans[0]]
        send((k, "a-", 0), mine, mine, at_x(-1))
        send((k, "c", 0), dl.at[c, core, x, low], dl.at[c, core, x, low], at_core())

    def stage_f(k):
        c, low = k // SUBS, k % SUBS
        left = dl.at[c, core, xof(-1), low, :, pl.ds(0, half)]
        arrive((k, "a+", 0), left)
        send((k, "a", 1), left, left, at_x(1))
        right = dl.at[c, core, xof(1), low, :, pl.ds(half, half)]
        arrive((k, "a-", 1), right)
        send((k, "a", -1), right, right, at_x(-1))

    def stage_c(k):
        c, low = k // SUBS, k % SUBS
        arrive((k, "a+", 1), dl.at[c, core, xof(-1), low, :, pl.ds(half, half)])
        send((k, "c", 1), dl.at[c, core, xof(-1), low], dl.at[c, core, xof(-1), low], at_core())
        arrive((k, "a-", 0), dl.at[c, core, xof(1), low, :, pl.ds(0, half)])
        send((k, "c", 3), dl.at[c, core, xof(1), low], dl.at[c, core, xof(1), low], at_core())
        arrive((k, "a", 1), dl.at[c, core, xof(2), low, :, pl.ds(0, half)])
        arrive((k, "a", -1), dl.at[c, core, xof(2), low, :, pl.ds(half, half)])
        send((k, "c", 2), dl.at[c, core, xof(2), low], dl.at[c, core, xof(2), low], at_core())

    def stage_p(k):
        arrive((SUBS * k, "c"), dl.at[k, 1 - core])
        bring(dl.at[k], dl_out.at[k])

        def step(i, carry):
            at = pl.ds(pl.multiple_of(i * PTILE, PTILE), PTILE)
            rows = dl[k].reshape(16 * ROWS, width)
            out = lax.dot_general(rows, head[at, :], (((1,), (1,)), ((), ())), preferred_element_type=F32)
            pg[k, :, :, :, :, at] = out.reshape(2, NZ, 2, ROWS, PTILE)
            pgs[k, :, :, :, :, at] = out.astype(jnp.bfloat16).reshape(2, NZ, 2, ROWS, PTILE)
            return carry

        lax.fori_loop(0, dhalf // PTILE, step, 0)
        for d in (1, 3, 2):
            yy = yof(d)
            src = pgs.at[k, lax.div(yy, 2), :, lax.rem(yy, 2), :, cols0]
            send((k, "g1y", d), src, ga.at[k, d - 1], at_y(d))
        lax.fori_loop(dhalf // PTILE, depth // PTILE, step, 0)
        for d in (1, 3, 2):
            src = pgs.at[k, :, zof(d), :, :, cols1]
            send((k, "g1z", d), src, gb.at[k, d - 1], at_z(d))

    def stage_h(k):
        grads = dl[:, :, :, :, :, pl.ds(width - EARLY, EARLY)].reshape(16 * ROWS * CHUNKS, EARLY)
        early[...] = jnp.dot(hid_t[...], grads, preferred_element_type=F32)
        bring(early, early_out)

    def stage_u(k):
        arrive((k, "g1y"), ga.at[k])
        value = pg[k, ycd, :, ylo, :, cols0]
        for d in range(3):
            value += ga[k, d].astype(F32)
        rsum[k, 0] = value
        for d in (1, 3, 2):
            send((k, "g2z", d), rsum.at[k, 0, zof(d)], gc.at[k, d - 1, 0], at_z(d))
        arrive((k, "g1z"), gb.at[k])
        value = pg[k, :, z, :, :, cols1]
        for d in range(3):
            value += gb[k, d].astype(F32)
        rsum[k, 1] = value.reshape(4, ROWS, dhalf)
        for d in (1, 3, 2):
            send((k, "g2y", d), rsum.at[k, 1, yof(d)], gc.at[k, d - 1, 1], at_y(d))

    def stage_v(k):
        rows = pl.ds(ROWS * k, ROWS)
        for j, (name, mine) in enumerate((("g2z", z), ("g2y", y))):
            value = rsum[k, j, mine]
            arrive((k, name), gc.at[k, :, j])
            for d in range(3):
                value += gc[k, d, j]
            hgrad_ref[rows, pl.ds(j * dhalf, dhalf)] = value

    stages = dict(
        A=stage_a, B=stage_b, M=stage_m, Q=stage_q, R=stage_r, L=stage_l, S=stage_s, T=stage_t,
        F=stage_f, C=stage_c, P=stage_p, H=stage_h, U=stage_u, V=stage_v,
    )
    for word in ORDER:
        with jax.named_scope("stage_" + word):
            stages[word[0]](int(word[1:]))
    three = pl.ds(0, 3)
    for name, view in (
        ("core0", part.at[0, 1 - core]), ("core1", part.at[1, 1 - core]),
        ("h1", dl.at[0, 0, three, 0]), ("h2", dl.at[three, 0, :, 0]),
        ("q1", q1s), ("q2", q2s), ("s", stat_r), ("g1y", ga), ("g1z", gb), ("g2", gc),
        ("c", dl.at[:, 1 - core]), ("a", dl.at[:, core, three]),
    ):
        sent(name, view)
    for copy in locals_[len(own) + len(head_loads) + 1 :]:
        copy.wait()


def head_kernel(
    rows_ref, grads_ref, early_ref, hidden_ref, hgrad_ref, out_ref, rows, grads, outs, early, hgrad, row_sem, in_sem, out_sem, pass_sem
):
    starts = [sum(SPANS[:i]) for i in range(len(SPANS))]
    spans = [pl.ds(at, size) for at, size in zip(starts, SPANS)]
    loads = [pltpu.make_async_copy(rows_ref, rows, row_sem.at[0])]
    loads += [
        pltpu.make_async_copy(grads_ref.at[:, span], grads.at[:, span], in_sem.at[i]) for i, span in enumerate(spans)
    ]
    loads[0].start()
    loads[1].start()
    loads[2].start()
    loads[0].wait()
    taken = [
        pltpu.make_async_copy(early_ref, early, pass_sem.at[0]),
        pltpu.make_async_copy(hidden_ref, hgrad, pass_sem.at[1]),
    ]
    passed = [
        pltpu.make_async_copy(early, out_ref.at[:, pl.ds(sum(SPANS), EARLY)], pass_sem.at[2]),
        pltpu.make_async_copy(hgrad, hgrad_ref, pass_sem.at[3]),
    ]
    stores = []
    for i, span in enumerate(spans):
        loads[1 + i].wait()
        if i == 0:
            for copy in taken:
                copy.start()
        if i == 1:
            for copy, last in zip(taken, passed):
                copy.wait()
                last.start()
        if i + 3 < len(loads):
            loads[i + 3].start()
        if i >= 2:
            stores[i - 2].wait()
        here = outs.at[i % 2, :, pl.ds(0, SPANS[i])]
        here[...] = jnp.dot(rows[...], grads[:, span], preferred_element_type=F32)
        stores.append(pltpu.make_async_copy(here, out_ref.at[:, span], out_sem.at[i]))
        stores[-1].start()
    for copy in stores[-2:] + passed:
        copy.wait()


def head_gradient(rows, grads, early, hidden_grad):
    (depth, tokens), width = rows.shape, grads.shape[1]
    any_space = pl.BlockSpec(memory_space=pl.ANY)
    return pl.pallas_call(
        head_kernel,
        out_shape=(
            jax.ShapeDtypeStruct(hidden_grad.shape, F32),
            jax.ShapeDtypeStruct((depth, width), F32),
        ),
        in_specs=[any_space] * 4,
        out_specs=(any_space, any_space),
        scratch_shapes=[
            pltpu.VMEM((depth, tokens), rows.dtype),
            pltpu.VMEM((tokens, width), grads.dtype),
            pltpu.VMEM((2, depth, max(SPANS)), F32),
            pltpu.VMEM((depth, EARLY), F32),
            pltpu.VMEM(hidden_grad.shape, F32),
            pltpu.SemaphoreType.DMA((1,)),
            pltpu.SemaphoreType.DMA((len(SPANS),)),
            pltpu.SemaphoreType.DMA((len(SPANS),)),
            pltpu.SemaphoreType.DMA((4,)),
        ],
        compiler_params=pltpu.CompilerParams(vmem_limit_bytes=56 * 1024 * 1024),
    )(rows, grads, early, hidden_grad)


def per_device(hidden, head, ref_logits, token_ids, group_ids, response_mask, advantages):
    depth, width = head.shape
    groups = advantages.shape[0]
    dhalf = depth // 2
    bf16, i16 = jnp.bfloat16, jnp.int16
    any_space = pl.BlockSpec(memory_space=pl.ANY)
    in_vmem = pl.BlockSpec(memory_space=pltpu.VMEM)
    hidden_grad, grads, rows, early = pl.pallas_call(
        kernel,
        out_shape=(
            jax.ShapeDtypeStruct((CHUNKS * ROWS, depth), F32),
            jax.ShapeDtypeStruct((CHUNKS, 2, NX, SUBS, ROWS, width), bf16),
            jax.ShapeDtypeStruct((depth, 16 * ROWS * CHUNKS), bf16),
            jax.ShapeDtypeStruct((depth, EARLY), F32),
        ),
        in_specs=[any_space] * 3 + [in_vmem] * 4,
        out_specs=(in_vmem, any_space, any_space, any_space),
        scratch_shapes=[
            pltpu.VMEM((depth, width), bf16),
            pltpu.VMEM((CHUNKS, 2, NZ, 2, ROWS, depth), bf16),
            pltpu.VMEM(ref_logits.shape, bf16),
            pltpu.VMEM((2, 2, NX, SUBS, ROWS, width), F32),
            pltpu.VMEM((CHUNKS, NX, SUBS, ROWS, width), F32),
            pltpu.VMEM((ROWS, width), F32),
            pltpu.VMEM((SUBS * CHUNKS, 2, ROWS, width // 2 + LANES), i16),
            pltpu.VMEM((SUBS * CHUNKS, 2, ROWS, width // 2 + LANES), i16),
            pltpu.VMEM((SUBS * CHUNKS, 2, ROWS, width + LANES), i16),
            pltpu.VMEM((SUBS * CHUNKS, 2, ROWS, width + LANES), i16),
            pltpu.VMEM((SUBS * CHUNKS, ROWS, width), F32),
            pltpu.VMEM((SUBS * CHUNKS, 2, ROWS, LANES), F32),
            pltpu.VMEM((SUBS * CHUNKS, 2, 3, ROWS, LANES), F32),
            pltpu.VMEM((CHUNKS, 2, NX, SUBS, ROWS, width), bf16),
            pltpu.VMEM((CHUNKS, 2, NZ, 2, ROWS, depth), F32),
            pltpu.VMEM((CHUNKS, 2, NZ, 2, ROWS, depth), bf16),
            pltpu.VMEM((CHUNKS, 3, 4, ROWS, dhalf), bf16),
            pltpu.VMEM((CHUNKS, 3, 2, 2, ROWS, dhalf), bf16),
            pltpu.VMEM((CHUNKS, 3, 2, ROWS, dhalf), F32),
            pltpu.VMEM((CHUNKS, 2, 4, ROWS, dhalf), F32),
            pltpu.VMEM((LANES, LANES), F32),
            pltpu.VMEM((LANES, LANES), F32),
            pltpu.VMEM((LANES, LANES), F32),
            pltpu.VMEM((depth, 16 * ROWS * CHUNKS), bf16),
            pltpu.VMEM((depth, EARLY), F32),
            pltpu.SemaphoreType.DMA((len(SENDERS),)),
            pltpu.SemaphoreType.DMA((34 * CHUNKS + 1,)),
            pltpu.SemaphoreType.DMA((20,)),
        ],
        compiler_params=pltpu.CompilerParams(
            collective_id=0, has_side_effects=True, vmem_limit_bytes=62 * 1024 * 1024
        ),
    )(
        hidden, head, ref_logits,
        token_ids.reshape(8, LANES), group_ids.reshape(8, LANES), response_mask.reshape(8, LANES),
        advantages.reshape(1, groups),
    )
    return head_gradient(rows, grads.reshape(-1, width), early, hidden_grad)


def solution(mesh):
    placed = (
        P("vocab", ("dp", "rows")),
        P(("dp", "rows"), "vocab"),
        P(("dp", "rows"), "vocab"),
        P(),
        P(),
        P(),
        P(),
    )
    return jax.shard_map(
        per_device,
        mesh=mesh,
        in_specs=placed,
        out_specs=(P("vocab", ("dp", "rows")), P(("dp", "rows"), "vocab")),
        check_vma=False,
    )
```

```python
import functools

import jax
import jax.numpy as jnp
from jax import lax
from jax.experimental import pallas as pl
from jax.experimental.pallas import tpu as pltpu
from jax.sharding import PartitionSpec as P

MESH = pl.DeviceIdType.MESH
CHUNKS = 4
NX = 4
NY = 4
NZ = 4
ROWS = 16
SUBS = 2
TILE = 2048
MTILE = 1024
PTILE = 512
LANES = 128
UNIT = 32000.0
F32 = jnp.float32
SPANS = (512, 1024, 1024, 512)
EARLY = 1024
SENDERS = ("core0", "core1", "h1", "h2", "q1", "q2", "s", "g1y", "g1z", "g2", "c", "a")

ORDER = (
    "A0", "B0", "A1", "B1", "M0", "Q0", "M1", "A2", "Q1", "R0", "B2", "R1", "A3", "Q2", "L0", "B3", "Q3",
    "R2", "S0", "L1", "R3", "M2", "T0", "S1", "L2", "Q4", "F0", "T1", "Q5", "L3", "R4", "M3", "S2", "S3",
    "F1", "Q6", "T2", "L4", "R5", "Q7", "C0", "C1", "R6", "S4", "P0", "T3", "L5", "F2", "R7", "L6", "S5",
    "F3", "T4", "S6", "T5", "C2", "L7", "T6", "C3", "U0", "S7", "F4", "P1", "F5", "T7", "V0", "C4", "C5",
    "F6", "U1", "F7", "P2", "C6", "C7", "P3", "H3", "U2", "V1", "U3", "V2", "V3",
)


def fold(values):
    return [values[:, j : j + LANES] for j in range(0, values.shape[1], LANES)]


def column(row):
    square = (LANES, LANES)
    same = lax.broadcasted_iota(jnp.int32, square, 0) == lax.broadcasted_iota(jnp.int32, square, 1)
    return jnp.sum(jnp.where(same, jnp.broadcast_to(row, square), 0.0), axis=1, keepdims=True)


def spread(columns):
    rows = columns[0].shape[0]
    lane = lax.broadcasted_iota(jnp.int32, (rows, LANES), 1)
    tile = jnp.zeros((rows, LANES), F32)
    for j, value in enumerate(columns):
        tile = jnp.where(lane == j, value, tile)
    return tile


def merge(tiles):
    get = lambda tile, j: tile[:, j : j + 1]
    top = functools.reduce(jnp.maximum, [get(t, 0) for t in tiles])
    qtop = functools.reduce(jnp.maximum, [get(t, 4) for t in tiles])
    scale = [jnp.exp(get(t, 0) - top) for t in tiles]
    qscale = [jnp.exp(get(t, 4) - qtop) for t in tiles]
    total, sum_z, sum_r = (sum(get(t, j) * s for t, s in zip(tiles, scale)) for j in (1, 2, 3))
    qtotal = sum(get(t, 5) * s for t, s in zip(tiles, qscale))
    return (top, total, sum_z, sum_r, qtop, qtotal)


def kernel(
    hidden_ref, head_ref, refs_ref, token_ref, group_ref, mask_ref, adv_ref,
    hgrad_ref, dl_out, hid_out, early_out,
    head, hid, refs, part, crecv, temp, q1s, q1r, q2s, q2r, zbuf, stat_s, stat_r, dl, pg, pgs, ga, gb, gc, rsum,
    tok_c, adv_c, wgt_c, hid_t, early, send_sem, recv_sem, local_sem,
):
    x = lax.axis_index("dp")
    core = lax.axis_index("rows")
    shard = lax.axis_index("vocab")
    y, z = lax.rem(shard, NY), lax.div(shard, NY)
    width = head.shape[1]
    half = width // 2
    depth = head.shape[0]
    dhalf = depth // 2
    block = 2 * x + core
    ycd, ylo = lax.div(y, 2), lax.rem(y, 2)

    def xof(step):
        return lax.rem(x + step + 2 * NX, NX)

    def yof(step):
        return lax.rem(y + step, NY)

    def zof(step):
        return lax.rem(z + step, NZ)

    def at_core():
        return {"rows": 1 - core}

    def at_x(step):
        return {"dp": xof(step)}

    def at_y(step):
        return {"vocab": z * NY + yof(step)}

    def at_z(step):
        return {"vocab": zof(step) * NY + y}

    numbers = {}

    def number(key):
        if key[1] in ("q1", "q2", "a+", "a-", "a"):
            return numbers.setdefault(key, len(numbers))
        if key[1] == "c":
            return numbers.setdefault((key[0] // SUBS, "c"), len(numbers))
        return numbers.setdefault(key[:2], len(numbers))

    def send(key, src, dst, device):
        name = key[1] + str(key[0] // SUBS % 2) if key[1] == "core" else key[1]
        n = next(i for i, start in enumerate(SENDERS) if name.startswith(start))
        pltpu.make_async_remote_copy(
            src_ref=src, dst_ref=dst, send_sem=send_sem.at[n], recv_sem=recv_sem.at[number(key)],
            device_id=device, device_id_type=MESH,
        ).start()

    def arrive(key, view):
        pltpu.make_async_copy(view, view, recv_sem.at[number(key)]).wait()

    def sent(name, view):
        pltpu.make_async_copy(view, view, send_sem.at[SENDERS.index(name)]).wait()

    locals_ = []

    def bring(src, dst):
        copy = pltpu.make_async_copy(src, dst, local_sem.at[len(locals_)])
        copy.start()
        locals_.append(copy)
        return copy

    own = [bring(hidden_ref.at[pl.ds(ROWS * k, ROWS)], hid.at[k, ycd, z, ylo]) for k in range(CHUNKS)]
    head_loads = [
        bring(head_ref.at[pl.ds(j * depth // 4, depth // 4)], head.at[pl.ds(j * depth // 4, depth // 4)])
        for j in range(4)
    ]
    refs_load = bring(refs_ref, refs)
    barrier = pltpu.get_barrier_semaphore()
    peers = [at_core(), at_x(1), at_x(-1)] + [at_y(d) for d in (1, 2, 3)] + [at_z(d) for d in (1, 2, 3)]
    for peer in peers:
        pl.semaphore_signal(barrier, inc=1, device_id=peer, device_id_type=MESH)
    pl.semaphore_wait(barrier, len(peers))

    cols0, cols1 = pl.ds(0, dhalf), pl.ds(dhalf, dhalf)
    def own_row(ref):
        values = ref[...].astype(F32)
        at = lax.broadcasted_iota(jnp.int32, values.shape, 0) == block
        return jnp.sum(jnp.where(at, values, 0.0), axis=0, keepdims=True)

    groups = adv_ref.shape[1]
    group_col = column(own_row(group_ref))
    group_at = lax.broadcasted_iota(jnp.int32, (LANES, groups), 1).astype(F32)
    adv_col = jnp.sum(jnp.where(group_col == group_at, adv_ref[...], 0.0), axis=1, keepdims=True)
    tok_c[...] = jnp.broadcast_to(column(own_row(token_ref)), tok_c.shape)
    adv_c[...] = jnp.broadcast_to(adv_col, adv_c.shape)
    wgt_c[...] = jnp.broadcast_to(column(own_row(mask_ref)), wgt_c.shape)

    def own_rows(ref, k, cols):
        at = 4 * ROWS * (k % SUBS) + ROWS * (k // SUBS)
        return ref[pl.ds(at, ROWS), cols].astype(F32)

    def tiles(lo, hi, body, init):
        def step(i, carry):
            return body(pl.multiple_of(i * TILE, TILE), carry)

        return lax.fori_loop(lo // TILE, hi // TILE, step, init)

    def exponent(top):
        return jnp.floor(jnp.log2(jnp.maximum(top, 1e-30))) + 1.0

    def code(values, by):
        return jnp.round(values * by).astype(jnp.int32).astype(jnp.int16)

    def decode(ref, cols, by):
        return ref[:, cols].astype(jnp.int32).astype(F32) * by

    def unit_of(ref, at):
        return jnp.exp2(ref[:, pl.ds(at, LANES)].astype(jnp.int32).astype(F32)[:, 0:1]) * (1.0 / UNIT)

    def local_sum(k, xd, cols):
        c, low = k // SUBS, k % SUBS
        return part[c % 2, core, xd, low, :, cols] + crecv[c, xd, low, :, cols]

    def stage_a(k):
        own[k].wait()
        for d in (1, 3, 2):
            mine = hid.at[k, ycd, z, ylo, :, cols0]
            send((k, "h1y", d), mine, mine, at_y(d))
            mine = hid.at[k, ycd, z, ylo, :, cols1]
            send((k, "h1z", d), mine, mine, at_z(d))

    def stage_b(k):
        arrive((k, "h1y"), dl.at[0, 0, pl.ds(0, 3), 0, :, cols0])
        arrive((k, "h1z"), dl.at[0, 0, pl.ds(0, 3), 0, :, cols0])
        for d in (1, 3, 2):
            mine = hid.at[k, :, z, :, :, cols0]
            send((k, "h2z", d), mine, mine, at_z(d))
            mine = hid.at[k, ycd, :, ylo, :, cols1]
            send((k, "h2y", d), mine, mine, at_y(d))

    def stage_m(k):
        if k == 0:
            for copy in head_loads:
                copy.wait()
        arrive((k, "h2z"), dl.at[0, :, pl.ds(0, 3), :, :, cols0])
        arrive((k, "h2y"), dl.at[0, :, pl.ds(0, 3), :, :, cols0])
        slot = k % 2
        hid_t[:, pl.ds(16 * ROWS * k, 16 * ROWS)] = jnp.swapaxes(hid[k].reshape(16 * ROWS, depth), 0, 1)
        if k == CHUNKS - 1:
            bring(hid_t, hid_out)
        if k >= 2:
            sent("core" + str(slot), part.at[slot, 1 - core])
        for lows in ((0,), (1,)) if k == 0 else ((0, 1),):
            low, many = pl.ds(lows[0], len(lows)), len(lows)
            for g in range(width // MTILE):
                cols = pl.ds(g * MTILE, MTILE)
                rows = hid[k, :, :, low].reshape(8 * many * ROWS, depth)
                out = jnp.dot(rows, head[:, cols], preferred_element_type=F32)
                part[slot, :, :, low, :, cols] = out.reshape(2, NX, many, ROWS, MTILE)
                src = part.at[slot, 1 - core, :, low, :, cols]
                send((SUBS * k + lows[0], "core", g), src, crecv.at[k, :, low, :, cols], at_core())

    def stage_q(k):
        if k < SUBS:
            arrive((k, "core"), crecv.at[0, :, k])
        elif k % SUBS == 0:
            arrive((k, "core"), crecv.at[k // SUBS])
        xd = xof(2)

        def first(at, top):
            cols = pl.ds(at, TILE)
            value = local_sum(k, xd, cols)
            temp[:, cols] = value
            return functools.reduce(jnp.maximum, fold(jnp.abs(value)), top)

        top = tiles(0, width, first, jnp.zeros((ROWS, LANES), F32))
        power = exponent(jnp.max(top, axis=1, keepdims=True))
        by = jnp.exp2(-power) * UNIT
        for j in range(2):

            def second(at, carry):
                q1s[k, j, :, pl.ds(pl.multiple_of(at - j * half, TILE), TILE)] = code(temp[:, pl.ds(at, TILE)], by)
                return carry

            tiles(j * half, (j + 1) * half, second, 0)
            q1s[k, j, :, pl.ds(half, LANES)] = jnp.broadcast_to(power, (ROWS, LANES)).astype(jnp.int32).astype(jnp.int16)
            send((k, "q1", j), q1s.at[k, j], q1r.at[k, j], at_x(1 if j == 0 else -1))

    def stage_r(k):
        for j in range(2):
            step = 1 if j == 0 else -1
            xd = xof(step)
            arrive((k, "q1", j), q1r.at[k, j])
            unit = unit_of(q1r.at[k, j], half)

            def plain(at, top):
                cols = pl.ds(at, TILE)
                value = local_sum(k, xd, cols)
                temp[:, cols] = value
                return functools.reduce(jnp.maximum, fold(jnp.abs(value)), top)

            def passing(at, top):
                cols = pl.ds(at, TILE)
                value = local_sum(k, xd, cols)
                value += decode(q1r.at[k, j], pl.ds(pl.multiple_of(at - j * half, TILE), TILE), unit)
                temp[:, cols] = value
                return functools.reduce(jnp.maximum, fold(jnp.abs(value)), top)

            top = tiles(j * half, (j + 1) * half, passing, jnp.zeros((ROWS, LANES), F32))
            top = tiles((1 - j) * half, (2 - j) * half, plain, top)
            power = exponent(jnp.max(top, axis=1, keepdims=True))
            by = jnp.exp2(-power) * UNIT

            def second(at, carry):
                cols = pl.ds(at, TILE)
                q2s[k, j, :, cols] = code(temp[:, cols], by)
                return carry

            tiles(0, width, second, 0)
            q2s[k, j, :, pl.ds(width, LANES)] = jnp.broadcast_to(power, (ROWS, LANES)).astype(jnp.int32).astype(jnp.int16)
            send((k, "q2", j), q2s.at[k, j], q2r.at[k, j], at_x(step))

    def stage_l(k):
        if k == 0:
            refs_load.wait()
        units = []
        for j in range(2):
            arrive((k, "q2", j), q2r.at[k, j])
            units.append(unit_of(q2r.at[k, j], width))

        def first(at, carry):
            top, qtop = carry
            cols = pl.ds(at, TILE)
            value = local_sum(k, x, cols)
            for j in range(2):
                value += decode(q2r.at[k, j], cols, units[j])
            zbuf[k, :, cols] = value
            top = functools.reduce(jnp.maximum, fold(value), top)
            qtop = functools.reduce(jnp.maximum, fold(own_rows(refs, k, cols)), qtop)
            return (top, qtop)

        low = jnp.full((ROWS, LANES), -jnp.inf, F32)
        top, qtop = tiles(0, width, first, (low, low))
        top = jnp.max(top, axis=1, keepdims=True)
        qtop = jnp.max(qtop, axis=1, keepdims=True)

        def second(at, carry):
            cols = pl.ds(at, TILE)
            value = zbuf[k, :, cols]
            ref = own_rows(refs, k, cols)
            expo = jnp.exp(value - top)
            adds = (expo, expo * value, expo * ref, jnp.exp(ref - qtop))
            return tuple(sum(fold(a), c) for a, c in zip(adds, carry))

        sums = tiles(0, width, second, (jnp.zeros((ROWS, LANES), F32),) * 4)
        total, sum_z, sum_r, qtotal = (jnp.sum(s, axis=1, keepdims=True) for s in sums)
        stat_s[k, 0] = spread((top, total, sum_z, sum_r, qtop, qtotal))
        for d in (1, 3, 2):
            send((k, "sy", d), stat_s.at[k, 0], stat_r.at[k, 0, d - 1], at_y(d))

    def stage_s(k):
        arrive((k, "sy"), stat_r.at[k, 0])
        stat_s[k, 1] = spread(merge([stat_s[k, 0]] + [stat_r[k, 0, d] for d in range(3)]))
        for d in (1, 3, 2):
            send((k, "sz", d), stat_s.at[k, 1], stat_r.at[k, 1, d - 1], at_z(d))

    def stage_t(k):
        c, low = k // SUBS, k % SUBS
        arrive((k, "sz"), stat_r.at[k, 1])
        top, total, sum_z, sum_r, qtop, qtotal = merge([stat_s[k, 1]] + [stat_r[k, 1, d] for d in range(3)])
        lse = top + jnp.log(total)
        qlse = qtop + jnp.log(qtotal)
        mean_z = sum_z / total
        mean_r = sum_r / total
        kl_term = mean_z - mean_r - lse + qlse
        entropy = lse - mean_z
        one = pl.ds(0, LANES)
        adv = own_rows(adv_c, k, one)[:, 0:1]
        weight = own_rows(wgt_c, k, one)[:, 0:1]
        base = adv + 0.04 * (qlse - lse - kl_term) + 0.02 * (entropy - lse)
        picked = weight * adv
        spot = own_rows(tok_c, k, one)[:, 0:1].astype(jnp.int32) - shard * width

        def body(at, carry):
            cols = pl.ds(at, TILE)
            value = zbuf[k, :, cols]
            ref = own_rows(refs, k, cols)
            grad = (weight * jnp.exp(value - lse)) * (base + 0.06 * value - 0.04 * ref)
            here = lax.broadcasted_iota(jnp.int32, (ROWS, TILE), 1) + at
            grad = grad - jnp.where(here == spot, picked, 0.0)
            dl[c, core, x, low, :, cols] = grad.astype(jnp.bfloat16)
            return carry

        spans = [pl.ds(0, half), pl.ds(half, half)]
        tiles(0, half, body, 0)
        mine = dl.at[c, core, x, low, :, spans[0]]
        send((k, "a+", 0), mine, mine, at_x(1))
        tiles(half, width, body, 0)
        mine = dl.at[c, core, x, low, :, spans[1]]
        send((k, "a-", 1), mine, mine, at_x(-1))
        send((k, "a+", 1), mine, mine, at_x(1))
        mine = dl.at[c, core, x, low, :, spans[0]]
        send((k, "a-", 0), mine, mine, at_x(-1))
        send((k, "c", 0), dl.at[c, core, x, low], dl.at[c, core, x, low], at_core())

    def stage_f(k):
        c, low = k // SUBS, k % SUBS
        left = dl.at[c, core, xof(-1), low, :, pl.ds(0, half)]
        arrive((k, "a+", 0), left)
        send((k, "a", 1), left, left, at_x(1))
        right = dl.at[c, core, xof(1), low, :, pl.ds(half, half)]
        arrive((k, "a-", 1), right)
        send((k, "a", -1), right, right, at_x(-1))

    def stage_c(k):
        c, low = k // SUBS, k % SUBS
        arrive((k, "a+", 1), dl.at[c, core, xof(-1), low, :, pl.ds(half, half)])
        send((k, "c", 1), dl.at[c, core, xof(-1), low], dl.at[c, core, xof(-1), low], at_core())
        arrive((k, "a-", 0), dl.at[c, core, xof(1), low, :, pl.ds(0, half)])
        send((k, "c", 3), dl.at[c, core, xof(1), low], dl.at[c, core, xof(1), low], at_core())
        arrive((k, "a", 1), dl.at[c, core, xof(2), low, :, pl.ds(0, half)])
        arrive((k, "a", -1), dl.at[c, core, xof(2), low, :, pl.ds(half, half)])
        send((k, "c", 2), dl.at[c, core, xof(2), low], dl.at[c, core, xof(2), low], at_core())

    def stage_p(k):
        arrive((SUBS * k, "c"), dl.at[k, 1 - core])
        bring(dl.at[k], dl_out.at[k])

        def step(i, carry):
            at = pl.ds(pl.multiple_of(i * PTILE, PTILE), PTILE)
            rows = dl[k].reshape(16 * ROWS, width)
            out = lax.dot_general(rows, head[at, :], (((1,), (1,)), ((), ())), preferred_element_type=F32)
            pg[k, :, :, :, :, at] = out.reshape(2, NZ, 2, ROWS, PTILE)
            pgs[k, :, :, :, :, at] = out.astype(jnp.bfloat16).reshape(2, NZ, 2, ROWS, PTILE)
            return carry

        lax.fori_loop(0, dhalf // PTILE, step, 0)
        for d in (1, 3, 2):
            yy = yof(d)
            src = pgs.at[k, lax.div(yy, 2), :, lax.rem(yy, 2), :, cols0]
            send((k, "g1y", d), src, ga.at[k, d - 1], at_y(d))
        lax.fori_loop(dhalf // PTILE, depth // PTILE, step, 0)
        for d in (1, 3, 2):
            src = pgs.at[k, :, zof(d), :, :, cols1]
            send((k, "g1z", d), src, gb.at[k, d - 1], at_z(d))

    def stage_h(k):
        grads = dl[:, :, :, :, :, pl.ds(width - EARLY, EARLY)].reshape(16 * ROWS * CHUNKS, EARLY)
        early[...] = jnp.dot(hid_t[...], grads, preferred_element_type=F32)
        bring(early, early_out)

    def stage_u(k):
        arrive((k, "g1y"), ga.at[k])
        value = pg[k, ycd, :, ylo, :, cols0]
        for d in range(3):
            value += ga[k, d].astype(F32)
        rsum[k, 0] = value
        for d in (1, 3, 2):
            send((k, "g2z", d), rsum.at[k, 0, zof(d)], gc.at[k, d - 1, 0], at_z(d))
        arrive((k, "g1z"), gb.at[k])
        value = pg[k, :, z, :, :, cols1]
        for d in range(3):
            value += gb[k, d].astype(F32)
        rsum[k, 1] = value.reshape(4, ROWS, dhalf)
        for d in (1, 3, 2):
            send((k, "g2y", d), rsum.at[k, 1, yof(d)], gc.at[k, d - 1, 1], at_y(d))

    def stage_v(k):
        rows = pl.ds(ROWS * k, ROWS)
        for j, (name, mine) in enumerate((("g2z", z), ("g2y", y))):
            value = rsum[k, j, mine]
            arrive((k, name), gc.at[k, :, j])
            for d in range(3):
                value += gc[k, d, j]
            hgrad_ref[rows, pl.ds(j * dhalf, dhalf)] = value

    stages = dict(
        A=stage_a, B=stage_b, M=stage_m, Q=stage_q, R=stage_r, L=stage_l, S=stage_s, T=stage_t,
        F=stage_f, C=stage_c, P=stage_p, H=stage_h, U=stage_u, V=stage_v,
    )
    for word in ORDER:
        with jax.named_scope("stage_" + word):
            stages[word[0]](int(word[1:]))
    three = pl.ds(0, 3)
    for name, view in (
        ("core0", part.at[0, 1 - core]), ("core1", part.at[1, 1 - core]),
        ("h1", dl.at[0, 0, three, 0]), ("h2", dl.at[three, 0, :, 0]),
        ("q1", q1s), ("q2", q2s), ("s", stat_r), ("g1y", ga), ("g1z", gb), ("g2", gc),
        ("c", dl.at[:, 1 - core]), ("a", dl.at[:, core, three]),
    ):
        sent(name, view)
    for copy in locals_[len(own) + len(head_loads) + 1 :]:
        copy.wait()


def head_kernel(
    rows_ref, grads_ref, early_ref, hidden_ref, hgrad_ref, out_ref, rows, grads, outs, early, hgrad, row_sem, in_sem, out_sem, pass_sem
):
    starts = [sum(SPANS[:i]) for i in range(len(SPANS))]
    spans = [pl.ds(at, size) for at, size in zip(starts, SPANS)]
    loads = [pltpu.make_async_copy(rows_ref, rows, row_sem.at[0])]
    loads += [
        pltpu.make_async_copy(grads_ref.at[:, span], grads.at[:, span], in_sem.at[i]) for i, span in enumerate(spans)
    ]
    loads[0].start()
    loads[1].start()
    loads[2].start()
    loads[0].wait()
    taken = [
        pltpu.make_async_copy(early_ref, early, pass_sem.at[0]),
        pltpu.make_async_copy(hidden_ref, hgrad, pass_sem.at[1]),
    ]
    passed = [
        pltpu.make_async_copy(early, out_ref.at[:, pl.ds(sum(SPANS), EARLY)], pass_sem.at[2]),
        pltpu.make_async_copy(hgrad, hgrad_ref, pass_sem.at[3]),
    ]
    stores = []
    for i, span in enumerate(spans):
        loads[1 + i].wait()
        if i == 0:
            for copy in taken:
                copy.start()
        if i + 3 < len(loads):
            loads[i + 3].start()
        if i >= 2:
            stores[i - 2].wait()
        here = outs.at[i % 2, :, pl.ds(0, SPANS[i])]
        here[...] = jnp.dot(rows[...], grads[:, span], preferred_element_type=F32)
        if i == 1:
            for copy, last in zip(taken, passed):
                copy.wait()
                last.start()
        stores.append(pltpu.make_async_copy(here, out_ref.at[:, span], out_sem.at[i]))
        stores[-1].start()
    for copy in stores[-2:] + passed:
        copy.wait()


def head_gradient(rows, grads, early, hidden_grad):
    (depth, tokens), width = rows.shape, grads.shape[1]
    any_space = pl.BlockSpec(memory_space=pl.ANY)
    return pl.pallas_call(
        head_kernel,
        out_shape=(
            jax.ShapeDtypeStruct(hidden_grad.shape, F32),
            jax.ShapeDtypeStruct((depth, width), F32),
        ),
        in_specs=[any_space] * 4,
        out_specs=(any_space, any_space),
        scratch_shapes=[
            pltpu.VMEM((depth, tokens), rows.dtype),
            pltpu.VMEM((tokens, width), grads.dtype),
            pltpu.VMEM((2, depth, max(SPANS)), F32),
            pltpu.VMEM((depth, EARLY), F32),
            pltpu.VMEM(hidden_grad.shape, F32),
            pltpu.SemaphoreType.DMA((1,)),
            pltpu.SemaphoreType.DMA((len(SPANS),)),
            pltpu.SemaphoreType.DMA((len(SPANS),)),
            pltpu.SemaphoreType.DMA((4,)),
        ],
        compiler_params=pltpu.CompilerParams(vmem_limit_bytes=56 * 1024 * 1024),
    )(rows, grads, early, hidden_grad)


def per_device(hidden, head, ref_logits, token_ids, group_ids, response_mask, advantages):
    depth, width = head.shape
    groups = advantages.shape[0]
    dhalf = depth // 2
    bf16, i16 = jnp.bfloat16, jnp.int16
    any_space = pl.BlockSpec(memory_space=pl.ANY)
    in_vmem = pl.BlockSpec(memory_space=pltpu.VMEM)
    hidden_grad, grads, rows, early = pl.pallas_call(
        kernel,
        out_shape=(
            jax.ShapeDtypeStruct((CHUNKS * ROWS, depth), F32),
            jax.ShapeDtypeStruct((CHUNKS, 2, NX, SUBS, ROWS, width), bf16),
            jax.ShapeDtypeStruct((depth, 16 * ROWS * CHUNKS), bf16),
            jax.ShapeDtypeStruct((depth, EARLY), F32),
        ),
        in_specs=[any_space] * 3 + [in_vmem] * 4,
        out_specs=(in_vmem, any_space, any_space, any_space),
        scratch_shapes=[
            pltpu.VMEM((depth, width), bf16),
            pltpu.VMEM((CHUNKS, 2, NZ, 2, ROWS, depth), bf16),
            pltpu.VMEM(ref_logits.shape, bf16),
            pltpu.VMEM((2, 2, NX, SUBS, ROWS, width), F32),
            pltpu.VMEM((CHUNKS, NX, SUBS, ROWS, width), F32),
            pltpu.VMEM((ROWS, width), F32),
            pltpu.VMEM((SUBS * CHUNKS, 2, ROWS, width // 2 + LANES), i16),
            pltpu.VMEM((SUBS * CHUNKS, 2, ROWS, width // 2 + LANES), i16),
            pltpu.VMEM((SUBS * CHUNKS, 2, ROWS, width + LANES), i16),
            pltpu.VMEM((SUBS * CHUNKS, 2, ROWS, width + LANES), i16),
            pltpu.VMEM((SUBS * CHUNKS, ROWS, width), F32),
            pltpu.VMEM((SUBS * CHUNKS, 2, ROWS, LANES), F32),
            pltpu.VMEM((SUBS * CHUNKS, 2, 3, ROWS, LANES), F32),
            pltpu.VMEM((CHUNKS, 2, NX, SUBS, ROWS, width), bf16),
            pltpu.VMEM((CHUNKS, 2, NZ, 2, ROWS, depth), F32),
            pltpu.VMEM((CHUNKS, 2, NZ, 2, ROWS, depth), bf16),
            pltpu.VMEM((CHUNKS, 3, 4, ROWS, dhalf), bf16),
            pltpu.VMEM((CHUNKS, 3, 2, 2, ROWS, dhalf), bf16),
            pltpu.VMEM((CHUNKS, 3, 2, ROWS, dhalf), F32),
            pltpu.VMEM((CHUNKS, 2, 4, ROWS, dhalf), F32),
            pltpu.VMEM((LANES, LANES), F32),
            pltpu.VMEM((LANES, LANES), F32),
            pltpu.VMEM((LANES, LANES), F32),
            pltpu.VMEM((depth, 16 * ROWS * CHUNKS), bf16),
            pltpu.VMEM((depth, EARLY), F32),
            pltpu.SemaphoreType.DMA((len(SENDERS),)),
            pltpu.SemaphoreType.DMA((34 * CHUNKS + 1,)),
            pltpu.SemaphoreType.DMA((20,)),
        ],
        compiler_params=pltpu.CompilerParams(
            collective_id=0, has_side_effects=True, vmem_limit_bytes=62 * 1024 * 1024
        ),
    )(
        hidden, head, ref_logits,
        token_ids.reshape(8, LANES), group_ids.reshape(8, LANES), response_mask.reshape(8, LANES),
        advantages.reshape(1, groups),
    )
    return head_gradient(rows, grads.reshape(-1, width), early, hidden_grad)


def solution(mesh):
    placed = (
        P("vocab", ("dp", "rows")),
        P(("dp", "rows"), "vocab"),
        P(("dp", "rows"), "vocab"),
        P(),
        P(),
        P(),
        P(),
    )
    return jax.shard_map(
        per_device,
        mesh=mesh,
        in_specs=placed,
        out_specs=(P("vocab", ("dp", "rows")), P(("dp", "rows"), "vocab")),
        check_vma=False,
    )
```
